32 devices in a mesh: sec: 4 (over x, core), seq: 8 (over z, y).
Axes of the slice: x: 2, y: 2, z: 4, core: 2. Of those that a mesh axis runs over, the one named last changes fastest.
Arguments:
- student_qkv: bfloat16 [1024, 3, 2560], P('seq', None, 'sec'), may hold values from -19 to 19
- target_qkv: bfloat16 [1024, 3, 2560], P('seq', None, 'sec'), may hold values from -19 to 19
- clip_lengths: int32 [4], replicated, may hold values from 1 to 384, 1024 in all
Outputs:
- student_grads: bfloat16 [1024, 3, 2560], P('seq', None, 'sec')
- target_out: bfloat16 [1024, 2560], P('seq', 'sec')
The draws below stay inside these ranges and needn't reach their ends.
Inputs may be any that keep to these rules, and one draw needn't show every extreme that they name: `clip_lengths`: the clip lengths sum to 1024, and the longest clip has exactly 384 tokens.
All inputs are finite; a program needn't handle non-finite values.
Results may differ from the reference program's by a relative error of at most 0.012.
Values may be sent and summed in bfloat16 or wider, within the bound.
No kernel may reach another device: no remote copies, remote signals or barrier semaphores. Data moves between devices by JAX's collectives and lax.ppermute only.
A program may use at most 64 MiB of HBM per device.

```python
import math
import jax
import jax.numpy as jnp
import numpy as np
from jax import lax

H = 20
HS = 128
TOK_DEV = 128
MOST = 384
TOKENS = 1024
NUM_CLIPS = 4


def views_helper(key, view_index):
    full_shape = (TOKENS, 3, H, HS)
    own_key = jax.random.fold_in(key, 11 + view_index)
    base_draw = jnp.clip(jax.random.normal(own_key, full_shape, jnp.float32), -3.0, 3.0)
    positions = jnp.arange(TOKENS, dtype=jnp.float32)
    roughness = jax.random.uniform(jax.random.fold_in(key, 21 + view_index), (TOKENS,), jnp.float32, 0.5, 1.5)
    token_scale = roughness * (1.0 + 2.0 * positions / max(TOKENS - 1, 1))
    head_scale = 0.7 + 0.7 * jnp.arange(H, dtype=jnp.float32) / max(H - 1, 1)
    query_part = base_draw[:, 0]
    key_part = base_draw[:, 1]
    values = base_draw[:, 2] * token_scale[:, None, None] * head_scale[None, :, None]
    stacked = jnp.stack([query_part, key_part, values], axis=1)
    return stacked.reshape(TOKENS, 3, H * HS)


def draw_student_qkv(key, part):
    return views_helper(key, 0).astype(jnp.bfloat16)


def draw_target_qkv(key, part):
    return views_helper(key, 1).astype(jnp.bfloat16)


def length_profile(count, total, reach, lean):
    weights = [(1 << 20) // math.isqrt(standing ** lean) + 1 for standing in range(2, count + 1)]
    surplus, counts = total - reach - (count - 1), [1] * (count - 1)
    while surplus > 0:
        movable = [i for i in range(count - 1) if counts[i] < reach]
        pool, remaining = sum([weights[i] for i in movable]), surplus
        for i in movable:
            addition = min(reach - counts[i], max(1, remaining * weights[i] // pool), surplus)
            counts[i] = counts[i] + addition
            surplus = surplus - addition
    return np.array([reach] + counts)


def uneven_parts(key, count, total, bound, skew):
    if count == 2:
        one = jax.random.randint(key, (), max(1, total - bound), min(bound, total - 1) + 1)
        return jnp.stack([one, total - one])
    lengths = jnp.asarray(length_profile(count, total, bound, skew), jnp.int32)
    pairs = (count - 1) // 2
    donor, sink = lengths[1:1 + 2 * pairs:2], lengths[2:2 + 2 * pairs:2]
    slack = jnp.minimum(donor - 1, bound - sink)
    passed = jax.random.randint(jax.random.fold_in(key, 1), (pairs,), 0, 1 << 20) % (slack + 1)
    lengths = lengths.at[1:1 + 2 * pairs:2].set(donor - passed).at[2:2 + 2 * pairs:2].set(sink + passed)
    return lengths[jax.random.permutation(jax.random.fold_in(key, 2), count)]


def setup_inputs(seed: int = 0) -> dict:
    key_list = jax.random.split(jax.random.key(seed), 4)
    student_qkv = draw_student_qkv(jax.random.fold_in(key_list[3], 71), 0)
    target_qkv = draw_target_qkv(jax.random.fold_in(key_list[3], 71), 0)
    clip_lengths = uneven_parts(key_list[2], NUM_CLIPS, TOKENS, MOST, 2).astype(jnp.int32)
    return {"student_qkv": student_qkv, "target_qkv": target_qkv, "clip_lengths": clip_lengths}


EPS = 1e-05
HIGHEST_PRECISION = lax.Precision.HIGHEST

def clip_ids(bounds, positions, total_rows):
    counted = jnp.searchsorted(bounds, positions, side='right').astype(jnp.int32)
    inside = (positions >= 0) & (positions < total_rows)
    local_index = jnp.arange(positions.shape[0], dtype=jnp.int32)
    return jnp.where(inside, counted, -1 - local_index)

def pad_rows(array, fill):
    widths = [(MOST, MOST)] + [(0, 0)] * (array.ndim - 1)
    return jnp.pad(array, widths, constant_values=fill)

def as_rounded(array):
    return lax.optimization_barrier(array.astype(jnp.bfloat16)).astype(jnp.float32)

def take_rows(array, first_row, count):
    return lax.dynamic_slice_in_dim(array, first_row, count, 0).astype(jnp.float32)

def reference(student_qkv, target_qkv, clip_lengths):
    token_count = student_qkv.shape[0]
    score_scale = 1.0 / math.sqrt(HS)
    bounds = jnp.cumsum(clip_lengths).astype(jnp.int32)
    window_rows = TOK_DEV + 2 * MOST
    block_ids = jnp.arange(token_count // TOK_DEV, dtype=jnp.int32)

    def masks_for(block_index):
        first_row = block_index * TOK_DEV
        own_ids = clip_ids(bounds, first_row + jnp.arange(TOK_DEV, dtype=jnp.int32), token_count)
        window_ids = clip_ids(bounds, first_row - MOST + jnp.arange(window_rows, dtype=jnp.int32), token_count)
        return (first_row, own_ids, window_ids)

    def heads_of(array):
        return array.reshape(array.shape[0], H, HS)

    def forward(view_rows):
        queries = heads_of(view_rows[:, 0])
        keys_padded = pad_rows(heads_of(view_rows[:, 1]), 0.0)
        values_padded = pad_rows(heads_of(view_rows[:, 2]), 0.0)

        def one_block(block_index):
            first_row, own_ids, window_ids = masks_for(block_index)
            allowed = own_ids[:, None] == window_ids[None, :]
            query_block = take_rows(queries, first_row, TOK_DEV)
            key_block = take_rows(keys_padded, first_row, window_rows)
            value_block = take_rows(values_padded, first_row, window_rows)
            scores = jnp.einsum('qhd,khd->hqk', query_block, key_block, precision=HIGHEST_PRECISION) * score_scale
            scores = jnp.where(allowed[None], scores, -jnp.inf)
            row_peak = lax.optimization_barrier(jnp.max(scores, axis=2))
            exponent = jnp.exp(scores - row_peak[:, :, None])
            row_total = lax.optimization_barrier(jnp.sum(exponent, axis=2))
            weights = as_rounded(exponent / row_total[:, :, None])
            output = jnp.einsum('hqk,khd->qhd', weights, value_block, precision=HIGHEST_PRECISION)
            return (output, row_peak.T, row_total.T)
        outputs, peaks, totals = lax.map(one_block, block_ids)
        return (outputs.reshape(token_count, H, HS), peaks.reshape(token_count, H), totals.reshape(token_count, H))
    student_out, student_peak, student_total = forward(student_qkv)
    target_out = forward(target_qkv)[0]
    difference = student_out - target_out
    row_squares = lax.optimization_barrier(jnp.sum(difference * difference, axis=(1, 2)))
    token_ids = clip_ids(bounds, jnp.arange(token_count, dtype=jnp.int32), token_count)
    clip_total = jax.ops.segment_sum(row_squares, token_ids, NUM_CLIPS)
    entries = clip_lengths.astype(jnp.float32) * (H * HS)
    factor = lax.rsqrt(clip_total / entries + EPS)
    out_grad = (difference * factor[token_ids][:, None, None]).astype(jnp.bfloat16)
    delta_sum = lax.optimization_barrier(jnp.sum(out_grad.astype(jnp.float32) * student_out, axis=2))
    queries = heads_of(student_qkv[:, 0])
    keys_all = heads_of(student_qkv[:, 1])
    values_all = heads_of(student_qkv[:, 2])
    queries_padded = pad_rows(queries, 0.0)
    keys_padded = pad_rows(keys_all, 0.0)
    values_padded = pad_rows(values_all, 0.0)
    grads_padded = pad_rows(out_grad, 0.0)
    peak_padded = pad_rows(student_peak, 0.0)
    total_padded = pad_rows(student_total, 1.0)
    delta_padded = pad_rows(delta_sum, 0.0)

    def backward_block(block_index):
        first_row, own_ids, window_ids = masks_for(block_index)
        own_mask = own_ids[:, None] == window_ids[None, :]
        key_mask = window_ids[:, None] == own_ids[None, :]
        query_own = take_rows(queries, first_row, TOK_DEV)
        grad_own = take_rows(out_grad, first_row, TOK_DEV)
        peak_own = take_rows(student_peak, first_row, TOK_DEV)
        total_own = take_rows(student_total, first_row, TOK_DEV)
        delta_own = take_rows(delta_sum, first_row, TOK_DEV)
        key_own = take_rows(keys_all, first_row, TOK_DEV)
        value_own = take_rows(values_all, first_row, TOK_DEV)
        key_window = take_rows(keys_padded, first_row, window_rows)
        value_window = take_rows(values_padded, first_row, window_rows)
        query_window = take_rows(queries_padded, first_row, window_rows)
        grad_window = take_rows(grads_padded, first_row, window_rows)
        peak_window = take_rows(peak_padded, first_row, window_rows)
        total_window = take_rows(total_padded, first_row, window_rows)
        delta_window = take_rows(delta_padded, first_row, window_rows)
        scores = jnp.einsum('qhd,khd->hqk', query_own, key_window, precision=HIGHEST_PRECISION) * score_scale
        scores = jnp.where(own_mask[None], scores, -jnp.inf)
        probability = jnp.exp(scores - peak_own.T[:, :, None]) / total_own.T[:, :, None]
        grad_prob = jnp.einsum('qhd,khd->hqk', grad_own, value_window, precision=HIGHEST_PRECISION)
        grad_score = as_rounded(probability * (grad_prob - delta_own.T[:, :, None]) * score_scale)
        grad_query = jnp.einsum('hqk,khd->qhd', grad_score, key_window, precision=HIGHEST_PRECISION)
        scores_keys = jnp.einsum('qhd,khd->hqk', query_window, key_own, precision=HIGHEST_PRECISION) * score_scale
        scores_keys = jnp.where(key_mask[None], scores_keys, -jnp.inf)
        prob_keys = jnp.exp(scores_keys - peak_window.T[:, :, None]) / total_window.T[:, :, None]
        weight_keys = as_rounded(prob_keys)
        grad_value = jnp.einsum('hqk,qhd->khd', weight_keys, grad_window, precision=HIGHEST_PRECISION)
        grad_prob_keys = jnp.einsum('qhd,khd->hqk', grad_window, value_own, precision=HIGHEST_PRECISION)
        grad_score_keys = as_rounded(prob_keys * (grad_prob_keys - delta_window.T[:, :, None]) * score_scale)
        grad_key = jnp.einsum('hqk,qhd->khd', grad_score_keys, query_window, precision=HIGHEST_PRECISION)
        return jnp.stack([grad_query, grad_key, grad_value], axis=1)
    gradients = lax.map(backward_block, block_ids)
    student_grads = gradients.reshape(token_count, 3, H * HS).astype(jnp.bfloat16)
    return (student_grads, target_out.astype(jnp.bfloat16).reshape(token_count, H * HS))
```

```python
import functools
import math

import jax
import jax.numpy as jnp
from jax import lax
from jax.experimental import pallas as pl
from jax.experimental.pallas import tpu as pltpu
from jax.sharding import PartitionSpec as P

H = 20
HS = 128
MOST = 384
EPS = 1e-05

GROUP = 8
OWNERS = ((0, 2, 4, 5, 7), (1, 2, 3, 5, 6))
ROUNDS = (4, 1, 5, 2, 6, 3, 7)
QUERY_TILE = 256
VMEM_BYTES = 48 * 1024 * 1024

BF16 = jnp.bfloat16
F32 = jnp.float32
ROWS_BY_ROWS = (((1,), (1,)), ((), ()))
VMEM = pl.BlockSpec(memory_space=pltpu.VMEM)
SMEM = pl.BlockSpec(memory_space=pltpu.SMEM)


def owner_code(owners):
    return sum((head + 1) << (3 * place) for head, place in enumerate(owners))


def place_and_code():
    place = lax.rem(lax.axis_index("seq"), GROUP)
    odd = lax.rem(lax.axis_index("sec"), 2) == 1
    code = jnp.where(odd, owner_code(OWNERS[1]), owner_code(OWNERS[0])).astype(jnp.int32)
    return place, code


def head_at(code, place):
    return lax.bitwise_and(lax.shift_right_logical(code, 3 * place), 7) - 1


def columns_of(head):
    return pl.ds(pl.multiple_of(head * HS, HS), HS)


def pack_kernel(student_ref, target_ref, *slots):
    place, code = place_and_code()
    for k in range(GROUP):
        head = head_at(code, lax.bitwise_xor(place, k))

        @pl.when(head >= 0)
        def _():
            slots[k][:3] = student_ref[:, :, columns_of(head)]
            slots[k][3:] = target_ref[:, :, columns_of(head)]


def clip_bounds(lengths_ref, count):
    bounds, total = [], jnp.int32(0)
    for clip in range(count):
        total = total + lengths_ref[clip]
        bounds.append(total)
    return bounds


def head_kernel(clip_count, extra, lengths_ref, *refs):
    slots = refs[: GROUP + extra]
    outs = refs[GROUP + extra : 2 * (GROUP + extra)]
    totals_ref, data, turned, ids_ref, grads = refs[2 * (GROUP + extra) :]
    place, code = place_and_code()
    rows = slots[0].shape[1]
    tokens = (GROUP + extra) * rows
    scale = 1.0 / math.sqrt(HS)
    to_log2 = scale * math.log2(math.e)
    totals_ref[...] = jnp.zeros_like(totals_ref)

    def rows_of(slot):
        block = lax.bitwise_xor(place, slot) if slot < GROUP else slot
        return pl.ds(pl.multiple_of(block * rows, rows), rows)

    @pl.when(head_at(code, place) >= 0)
    def _():
        group_start = lax.div(lax.axis_index("seq"), GROUP) * (GROUP * rows)
        bounds = clip_bounds(lengths_ref, clip_count)
        for slot in range(GROUP + extra):
            where = rows_of(slot)
            for part in range(6):
                data[part, where, :] = slots[slot][part]
            for turn, part in enumerate((1, 2, 5)):
                turned[turn, :, where] = slots[slot][part].T
        key_place = group_start + lax.broadcasted_iota(jnp.int32, (tokens, HS), 0)
        query_place = group_start + lax.broadcasted_iota(jnp.int32, (1, tokens), 1)
        key_ids = jnp.zeros((tokens, HS), jnp.int32)
        query_ids = jnp.zeros((1, tokens), jnp.int32)
        query_first = jnp.zeros((1, tokens), jnp.int32)
        for bound in bounds:
            key_ids = key_ids + (key_place >= bound).astype(jnp.int32)
            query_ids = query_ids + (query_place >= bound).astype(jnp.int32)
            query_first = jnp.where(query_place >= bound, bound, query_first)
        ids_ref[...] = key_ids
        owned = (query_first >= group_start) & (query_first < group_start + GROUP * rows)
        grads[1] = jnp.zeros((tokens, HS), F32)
        grads[2] = jnp.zeros((tokens, HS), F32)
        clip_iota = lax.broadcasted_iota(jnp.int32, (totals_ref.shape[0], 1), 0)

        def attend(part, turn, mine, keys, allowed):
            scores = lax.dot_general(
                data[part + 1, keys, :], data[part, mine, :], ROWS_BY_ROWS, preferred_element_type=F32
            )
            scores = jnp.where(allowed, scores, -jnp.inf)
            peak = jnp.max(scores, axis=0, keepdims=True)
            exponent = jnp.exp2((scores - peak) * to_log2)
            inverse = 1.0 / jnp.sum(exponent, axis=0, keepdims=True)
            weights = exponent.astype(BF16)
            out = jnp.dot(turned[turn, :, keys], weights, preferred_element_type=F32) * inverse
            return out, exponent, weights, inverse

        for first in range(0, tokens, QUERY_TILE):
            width = min(QUERY_TILE, tokens - first)
            mine = slice(first, first + width)
            keys = slice(max(0, first - MOST), min(tokens, first + width + MOST))
            key_tile = ids_ref[keys, :]
            key_tile = jnp.concatenate([key_tile] * (width // HS), axis=1)
            allowed = key_tile == query_ids[:, mine]
            target, _, _, _ = attend(3, 2, mine, keys, allowed)
            student, exponent, weights, inverse = attend(0, 1, mine, keys, allowed)
            diff = student - target
            if extra:
                diff = jnp.where(owned[:, mine], diff, 0.0)
                target = jnp.where(owned[:, mine], target, 0.0)
            squares = jnp.sum(diff * diff, axis=0, keepdims=True)
            counted = jnp.where(clip_iota == query_ids[:, mine], squares, 0.0)
            totals_ref[...] += jnp.sum(counted, axis=1, keepdims=True)
            gradient = (diff * inverse).astype(BF16)
            delta = jnp.sum(gradient.astype(F32) * student, axis=0, keepdims=True)
            slope = jnp.dot(data[2, keys, :], gradient, preferred_element_type=F32)
            dscores = (exponent * (slope - delta)).astype(BF16)
            dquery = jnp.dot(turned[0, :, keys], dscores, preferred_element_type=F32)
            grads[0, mine, :] = (dquery * scale).T
            grads[1, keys, :] += jnp.dot(dscores, data[0, mine, :], preferred_element_type=F32)
            grads[2, keys, :] += lax.dot_general(
                weights, gradient, ROWS_BY_ROWS, preferred_element_type=F32
            )
            grads[3, mine, :] = target.T
        for slot in range(GROUP + extra):
            where = rows_of(slot)
            outs[slot][0] = grads[0, where, :].astype(BF16)
            outs[slot][1] = (grads[1, where, :] * scale).astype(BF16)
            outs[slot][2] = grads[2, where, :].astype(BF16)
            outs[slot][3] = grads[3, where, :].astype(BF16)


def finish_kernel(clip_count, head_count, extra, lengths_ref, totals_ref, *refs):
    slots, extras, (grads_ref, target_ref) = refs[:GROUP], refs[GROUP:-2], refs[-2:]
    place, code = place_and_code()
    rows = slots[0].shape[1]
    first = lax.axis_index("seq") * rows
    token = first + lax.broadcasted_iota(jnp.int32, (rows, HS), 0)
    factor = jnp.zeros((rows, HS), F32)
    begin = jnp.int32(0)
    for clip in range(clip_count):
        length = lengths_ref[clip]
        size = length.astype(F32) * (H * HS)
        value = lax.rsqrt(totals_ref[clip : clip + 1, :] / size + EPS)
        factor = jnp.where((token >= begin) & (token < begin + length), value, factor)
        begin = begin + length
    for k in range(GROUP):
        head = head_at(code, lax.bitwise_xor(place, k))

        @pl.when(head >= 0)
        def _():
            cols = columns_of(head)
            for part in range(3):
                grads_ref[part, :, cols] = (slots[k][part].astype(F32) * factor).astype(BF16)
            target_ref[:, cols] = slots[k][3]

    for head in range(head_count if extra else 0):
        cols = slice(head * HS, (head + 1) * HS)
        for part in range(3):
            more = (extras[head][part].astype(F32) * factor).astype(BF16)
            grads_ref[part, :, cols] = grads_ref[part, :, cols] + more
        target_ref[:, cols] = target_ref[:, cols] + extras[head][3]


def both_axes(sec_count, seq_count, pairs_of):
    pairs = []
    for sec in range(sec_count):
        for start in range(0, seq_count, GROUP):
            for source, target in pairs_of(OWNERS[sec % 2], start):
                if source < seq_count and target < seq_count:
                    pairs.append((sec * seq_count + source, sec * seq_count + target))
    return pairs


def per_device(sec_count, seq_count, student_qkv, target_qkv, clip_lengths):
    rows, _, width = student_qkv.shape
    head_count = width // HS
    clip_count = clip_lengths.shape[0]
    total_rows = -(-clip_count // 8) * 8
    extra = MOST // rows if seq_count > GROUP else 0
    axes = ("sec", "seq")
    pairs = functools.partial(both_axes, sec_count, seq_count)
    params = pltpu.CompilerParams(vmem_limit_bytes=VMEM_BYTES)

    packed = pl.pallas_call(
        pack_kernel,
        out_shape=[jax.ShapeDtypeStruct((6, rows, HS), BF16)] * GROUP,
        in_specs=[VMEM] * 2,
        out_specs=[VMEM] * GROUP,
        compiler_params=params,
        name="pack",
    )(jnp.transpose(student_qkv, (1, 0, 2)), jnp.transpose(target_qkv, (1, 0, 2)))

    gathered = [packed[0]] + [None] * (GROUP - 1)
    for k in ROUNDS:
        gathered[k] = lax.ppermute(
            packed[k], axes, pairs(lambda owners, start: [(start + (d ^ k), start + d) for d in owners])
        )
    for block in range(extra):
        pieces = []
        for head in range(head_count):
            cols = slice(head * HS, (head + 1) * HS)
            piece = jnp.concatenate([student_qkv[:, :, cols], target_qkv[:, :, cols]], axis=1)
            pieces.append(
                lax.ppermute(
                    jnp.transpose(piece, (1, 0, 2)),
                    axes,
                    pairs(lambda owners, start: [(start + GROUP + block, start + owners[head])]),
                )
            )
        gathered.append(sum(pieces[1:], pieces[0]))

    tokens = (GROUP + extra) * rows
    *results, totals = pl.pallas_call(
        functools.partial(head_kernel, clip_count, extra),
        out_shape=[jax.ShapeDtypeStruct((4, rows, HS), BF16)] * (GROUP + extra)
        + [jax.ShapeDtypeStruct((total_rows, HS), F32)],
        in_specs=[SMEM] + [VMEM] * (GROUP + extra),
        out_specs=[VMEM] * (GROUP + extra + 1),
        scratch_shapes=[
            pltpu.VMEM((6, tokens, HS), BF16),
            pltpu.VMEM((3, HS, tokens), BF16),
            pltpu.VMEM((tokens, HS), jnp.int32),
            pltpu.VMEM((4, tokens, HS), F32),
        ],
        compiler_params=params,
        name="heads",
    )(clip_lengths, *gathered)

    returned = [results[0]] + [None] * (GROUP - 1)
    for k in ROUNDS:
        returned[k] = lax.ppermute(
            results[k], axes, pairs(lambda owners, start: [(start + d, start + (d ^ k)) for d in owners])
        )
    extras = []
    for head in range(head_count if extra else 0):
        pieces = [
            lax.ppermute(
                results[GROUP + block],
                axes,
                pairs(lambda owners, start: [(start + owners[head], start + GROUP + block)]),
            )
            for block in range(extra)
        ]
        extras.append(sum(pieces[1:], pieces[0]))
    for axis, count in (("sec", sec_count), ("seq", seq_count)):
        step = 1
        while step < count:
            totals = totals + lax.ppermute(totals, axis, [(s, s ^ step) for s in range(count)])
            step *= 2

    grads, target_out = pl.pallas_call(
        functools.partial(finish_kernel, clip_count, head_count, extra),
        out_shape=[
            jax.ShapeDtypeStruct((3, rows, width), BF16),
            jax.ShapeDtypeStruct((rows, width), BF16),
        ],
        in_specs=[SMEM] + [VMEM] * (1 + GROUP + len(extras)),
        out_specs=[VMEM] * 2,
        compiler_params=params,
        name="finish",
    )(clip_lengths, totals, *returned, *extras)
    return jnp.transpose(grads, (1, 0, 2)), target_out


def solution(mesh):
    return jax.shard_map(
        functools.partial(per_device, mesh.shape["sec"], mesh.shape["seq"]),
        mesh=mesh,
        in_specs=(P("seq", None, "sec"), P("seq", None, "sec"), P()),
        out_specs=(P("seq", None, "sec"), P("seq", "sec")),
        check_vma=False,
    )
```

```python
import functools
import math

import jax
import jax.numpy as jnp
from jax import lax
from jax.experimental import pallas as pl
from jax.experimental.pallas import tpu as pltpu
from jax.sharding import PartitionSpec as P

H = 20
HS = 128
MOST = 384
EPS = 1e-05

GROUP = 8
OWNERS = ((0, 2, 4, 5, 7), (1, 2, 3, 5, 6))
ROUNDS_IN = (4, 3, 5, 1, 7, 6, 2)
ROUNDS_OUT = (4, 3, 5, 7, 6, 2, 1)
QUERY_TILE = 256
HEADS_VMEM = 40 * 1024 * 1024
SMALL_VMEM = 8 * 1024 * 1024

BF16 = jnp.bfloat16
F32 = jnp.float32
ROWS_BY_ROWS = (((1,), (1,)), ((), ()))
VMEM = pl.BlockSpec(memory_space=pltpu.VMEM)
SMEM = pl.BlockSpec(memory_space=pltpu.SMEM)


def owner_code(owners):
    return sum((head + 1) << (3 * place) for head, place in enumerate(owners))


def place_and_code():
    place = lax.rem(lax.axis_index("seq"), GROUP)
    odd = lax.rem(lax.axis_index("sec"), 2) == 1
    code = jnp.where(odd, owner_code(OWNERS[1]), owner_code(OWNERS[0])).astype(jnp.int32)
    return place, code


def head_at(code, place):
    return lax.bitwise_and(lax.shift_right_logical(code, 3 * place), 7) - 1


def columns_of(head):
    return pl.ds(pl.multiple_of(head * HS, HS), HS)


def pack_kernel(student_ref, target_ref, *refs):
    slots, sems = in_slot_order(refs, ROUNDS_IN), refs[GROUP]
    place, code = place_and_code()

    def copies(k, head):
        return [
            pltpu.make_async_copy(
                view.at[:, :, columns_of(head)], slots[k].at[pl.ds(3 * i, 3)], sems.at[k, i]
            )
            for i, view in enumerate((student_ref, target_ref))
        ]

    for step in ("start", "wait"):
        for k in ROUNDS_IN + (0,):
            head = head_at(code, lax.bitwise_xor(place, k))

            @pl.when(head >= 0)
            def _():
                for copy in copies(k, head):
                    copy.start() if step == "start" else copy.wait()


def in_slot_order(refs, rounds):
    return [refs[((0,) + rounds).index(k)] for k in range(GROUP)]


def clip_bounds(lengths_ref, count):
    bounds, total = [], jnp.int32(0)
    for clip in range(count):
        total = total + lengths_ref[clip]
        bounds.append(total)
    return bounds


def head_kernel(clip_count, extra, lengths_ref, *refs):
    slots = in_slot_order(refs, ROUNDS_IN) + list(refs[GROUP : GROUP + extra])
    refs = refs[GROUP + extra :]
    outs = in_slot_order(refs, ROUNDS_OUT) + list(refs[GROUP : GROUP + extra])
    data, turned, ids_ref, grads, totals_ref = refs[GROUP + extra :]
    place, code = place_and_code()
    rows = slots[0].shape[1]
    tokens = (GROUP + extra) * rows
    scale = 1.0 / math.sqrt(HS)
    to_log2 = scale * math.log2(math.e)
    totals_ref[...] = jnp.zeros_like(totals_ref)
    clip_rows = totals_ref.shape[0]
    outs[0][4 * rows :] = jnp.zeros((2 * clip_rows, HS), BF16)

    def rows_of(slot):
        block = lax.bitwise_xor(place, slot) if slot < GROUP else slot
        return pl.ds(pl.multiple_of(block * rows, rows), rows)

    @pl.when(head_at(code, place) >= 0)
    def _():
        group_start = lax.div(lax.axis_index("seq"), GROUP) * (GROUP * rows)
        bounds = clip_bounds(lengths_ref, clip_count)
        for slot in range(GROUP + extra):
            where = rows_of(slot)
            for part in range(6):
                data[part, where, :] = slots[slot][part]
            for turn, part in enumerate((1, 2, 5)):
                turned[turn, :, where] = slots[slot][part].T
        key_place = group_start + lax.broadcasted_iota(jnp.int32, (tokens, HS), 0)
        query_place = group_start + lax.broadcasted_iota(jnp.int32, (1, tokens), 1)
        key_ids = jnp.zeros((tokens, HS), jnp.int32)
        query_ids = jnp.zeros((1, tokens), jnp.int32)
        query_first = jnp.zeros((1, tokens), jnp.int32)
        for bound in bounds:
            key_ids = key_ids + (key_place >= bound).astype(jnp.int32)
            query_ids = query_ids + (query_place >= bound).astype(jnp.int32)
            query_first = jnp.where(query_place >= bound, bound, query_first)
        ids_ref[...] = key_ids
        owned = (query_first >= group_start) & (query_first < group_start + GROUP * rows)
        grads[1] = jnp.zeros((tokens, HS), F32)
        grads[2] = jnp.zeros((tokens, HS), F32)
        clip_iota = lax.broadcasted_iota(jnp.int32, (totals_ref.shape[0], 1), 0)

        def attend(part, turn, mine, keys, allowed):
            scores = lax.dot_general(
                data[part + 1, keys, :], data[part, mine, :], ROWS_BY_ROWS, preferred_element_type=F32
            )
            scores = jnp.where(allowed, scores, -jnp.inf)
            peak = jnp.max(scores, axis=0, keepdims=True)
            exponent = jnp.exp2((scores - peak) * to_log2)
            inverse = 1.0 / jnp.sum(exponent, axis=0, keepdims=True)
            weights = exponent.astype(BF16)
            out = jnp.dot(turned[turn, :, keys], weights, preferred_element_type=F32) * inverse
            return out, exponent, weights, inverse

        for first in range(0, tokens, QUERY_TILE):
            width = min(QUERY_TILE, tokens - first)
            mine = slice(first, first + width)
            keys = slice(max(0, first - MOST), min(tokens, first + width + MOST))
            key_tile = ids_ref[keys, :]
            key_tile = jnp.concatenate([key_tile] * (width // HS), axis=1)
            allowed = key_tile == query_ids[:, mine]
            target, _, _, _ = attend(3, 2, mine, keys, allowed)
            student, exponent, weights, inverse = attend(0, 1, mine, keys, allowed)
            diff = student - target
            if extra:
                diff = jnp.where(owned[:, mine], diff, 0.0)
                target = jnp.where(owned[:, mine], target, 0.0)
            squares = jnp.sum(diff * diff, axis=0, keepdims=True)
            counted = jnp.where(clip_iota == query_ids[:, mine], squares, 0.0)
            totals_ref[...] += jnp.sum(counted, axis=1, keepdims=True)
            gradient = (diff * inverse).astype(BF16)
            delta = jnp.sum(gradient.astype(F32) * student, axis=0, keepdims=True)
            slope = jnp.dot(data[2, keys, :], gradient, preferred_element_type=F32)
            dscores = (exponent * (slope - delta)).astype(BF16)
            dquery = jnp.dot(turned[0, :, keys], dscores, preferred_element_type=F32)
            grads[0, mine, :] = (dquery * scale).T
            grads[1, keys, :] += jnp.dot(dscores, data[0, mine, :], preferred_element_type=F32)
            grads[2, keys, :] += lax.dot_general(
                weights, gradient, ROWS_BY_ROWS, preferred_element_type=F32
            )
            grads[3, mine, :] = target.T
        high = totals_ref[...].astype(BF16)
        low = (totals_ref[...] - high.astype(F32)).astype(BF16)
        for slot in range(GROUP + extra):
            where = rows_of(slot)
            for part, factor in enumerate((1.0, scale, 1.0, 1.0)):
                block = grads[part, where, :]
                block = block if factor == 1.0 else block * factor
                outs[slot][part * rows : (part + 1) * rows] = block.astype(BF16)
            outs[slot][4 * rows : 4 * rows + clip_rows] = high
            outs[slot][4 * rows + clip_rows :] = low


def sum_kernel(*refs):
    out = refs[-1]
    clip_rows = out.shape[0]
    total = jnp.zeros(out.shape, F32)
    for slot in refs[:-1]:
        start = slot.shape[0] - 2 * clip_rows
        total = total + slot[start : start + clip_rows].astype(F32)
        total = total + slot[start + clip_rows :].astype(F32)
    out[...] = total


def finish_kernel(clip_count, head_count, extra, lengths_ref, mine_ref, other_ref, *refs):
    slots, extras, (grads_ref, target_ref) = in_slot_order(refs, ROUNDS_OUT), refs[GROUP:-2], refs[-2:]
    place, code = place_and_code()
    rows = target_ref.shape[0]
    totals = mine_ref[...] + other_ref[...]
    first = lax.axis_index("seq") * rows
    token = first + lax.broadcasted_iota(jnp.int32, (rows, HS), 0)
    factor = jnp.zeros((rows, HS), F32)
    begin = jnp.int32(0)
    for clip in range(clip_count):
        length = lengths_ref[clip]
        size = length.astype(F32) * (H * HS)
        value = lax.rsqrt(totals[clip : clip + 1, :] / size + EPS)
        factor = jnp.where((token >= begin) & (token < begin + length), value, factor)
        begin = begin + length
    for k in range(GROUP):
        head = head_at(code, lax.bitwise_xor(place, k))

        @pl.when(head >= 0)
        def _():
            cols = columns_of(head)
            for part in range(3):
                block = slots[k][part * rows : (part + 1) * rows].astype(F32)
                grads_ref[part, :, cols] = (block * factor).astype(BF16)
            target_ref[:, cols] = slots[k][3 * rows : 4 * rows]

    for head in range(head_count if extra else 0):
        cols = slice(head * HS, (head + 1) * HS)
        for part in range(3):
            more = extras[head][part * rows : (part + 1) * rows].astype(F32)
            more = (more * factor).astype(BF16)
            grads_ref[part, :, cols] = grads_ref[part, :, cols] + more
        target_ref[:, cols] = target_ref[:, cols] + extras[head][3 * rows : 4 * rows]


def both_axes(sec_count, seq_count, pairs_of):
    pairs = []
    for sec in range(sec_count):
        for start in range(0, seq_count, GROUP):
            for source, target in pairs_of(OWNERS[sec % 2], start):
                if source < seq_count and target < seq_count:
                    pairs.append((sec * seq_count + source, sec * seq_count + target))
    return pairs


def per_device(sec_count, seq_count, student_qkv, target_qkv, clip_lengths):
    rows, _, width = student_qkv.shape
    head_count = width // HS
    clip_count = clip_lengths.shape[0]
    clip_rows = -(-clip_count // 8) * 8
    extra = MOST // rows if seq_count > GROUP else 0
    axes = ("sec", "seq")
    pairs = functools.partial(both_axes, sec_count, seq_count)
    small = pltpu.CompilerParams(vmem_limit_bytes=SMALL_VMEM)

    packed = pl.pallas_call(
        pack_kernel,
        out_shape=[jax.ShapeDtypeStruct((6, rows, HS), BF16)] * GROUP,
        in_specs=[pl.BlockSpec(memory_space=pltpu.HBM)] * 2,
        out_specs=[VMEM] * GROUP,
        scratch_shapes=[pltpu.SemaphoreType.DMA((GROUP, 2))],
        compiler_params=small,
        name="pack",
    )(jnp.transpose(student_qkv, (1, 0, 2)), jnp.transpose(target_qkv, (1, 0, 2)))

    gathered = [packed[0]]
    for k, mine in zip(ROUNDS_IN, packed[1:]):
        gathered.append(
            lax.ppermute(
                mine, axes, pairs(lambda owners, start: [(start + (d ^ k), start + d) for d in owners])
            )
        )
    for block in range(extra):
        pieces = []
        for head in range(head_count):
            cols = slice(head * HS, (head + 1) * HS)
            piece = jnp.concatenate([student_qkv[:, :, cols], target_qkv[:, :, cols]], axis=1)
            pieces.append(
                lax.ppermute(
                    jnp.transpose(piece, (1, 0, 2)),
                    axes,
                    pairs(lambda owners, start: [(start + GROUP + block, start + owners[head])]),
                )
            )
        gathered.append(sum(pieces[1:], pieces[0]))

    tokens = (GROUP + extra) * rows
    payload = jax.ShapeDtypeStruct((4 * rows + 2 * clip_rows, HS), BF16)
    results = pl.pallas_call(
        functools.partial(head_kernel, clip_count, extra),
        out_shape=[payload] * (GROUP + extra),
        in_specs=[SMEM] + [VMEM] * (GROUP + extra),
        out_specs=[VMEM] * (GROUP + extra),
        scratch_shapes=[
            pltpu.VMEM((6, tokens, HS), BF16),
            pltpu.VMEM((3, HS, tokens), BF16),
            pltpu.VMEM((tokens, HS), jnp.int32),
            pltpu.VMEM((4, tokens, HS), F32),
            pltpu.VMEM((clip_rows, HS), F32),
        ],
        compiler_params=pltpu.CompilerParams(vmem_limit_bytes=HEADS_VMEM),
        name="heads",
    )(clip_lengths, *gathered)

    returned = [results[0]]
    for k, mine in zip(ROUNDS_OUT, results[1:]):
        returned.append(
            lax.ppermute(
                mine, axes, pairs(lambda owners, start: [(start + d, start + (d ^ k)) for d in owners])
            )
        )
    extras = []
    for head in range(head_count if extra else 0):
        pieces = [
            lax.ppermute(
                results[GROUP + block],
                axes,
                pairs(lambda owners, start: [(start + owners[head], start + GROUP + block)]),
            )
            for block in range(extra)
        ]
        extras.append(sum(pieces[1:], pieces[0]))
    totals = pl.pallas_call(
        sum_kernel,
        out_shape=jax.ShapeDtypeStruct((clip_rows, HS), F32),
        in_specs=[VMEM] * GROUP,
        out_specs=VMEM,
        compiler_params=small,
        name="totals",
    )(*returned)

    def over(totals, axis, count, step):
        return lax.ppermute(totals, axis, [(s, s ^ step) for s in range(count)])

    step = GROUP
    while step < seq_count:
        totals = totals + over(totals, "seq", seq_count, step)
        step *= 2
    step = 1
    while 2 * step < sec_count:
        totals = totals + over(totals, "sec", sec_count, step)
        step *= 2

    grads, target_out = pl.pallas_call(
        functools.partial(finish_kernel, clip_count, head_count, extra),
        out_shape=[
            jax.ShapeDtypeStruct((3, rows, width), BF16),
            jax.ShapeDtypeStruct((rows, width), BF16),
        ],
        in_specs=[SMEM] + [VMEM] * (2 + GROUP + len(extras)),
        out_specs=[VMEM] * 2,
        compiler_params=small,
        name="finish",
    )(clip_lengths, totals, over(totals, "sec", sec_count, step), *returned, *extras)
    return jnp.transpose(grads, (1, 0, 2)), target_out


def solution(mesh):
    return jax.shard_map(
        functools.partial(per_device, mesh.shape["sec"], mesh.shape["seq"]),
        mesh=mesh,
        in_specs=(P("seq", None, "sec"), P("seq", None, "sec"), P()),
        out_specs=(P("seq", None, "sec"), P("seq", "sec")),
        check_vma=False,
    )
```

```python
import functools
import math

import jax
import jax.numpy as jnp
from jax import lax
from jax.experimental import pallas as pl
from jax.experimental.pallas import tpu as pltpu
from jax.sharding import PartitionSpec as P

H = 20
HS = 128
MOST = 384
EPS = 1e-05

GROUP = 8
OWNERS = ((0, 2, 4, 5, 7), (1, 2, 3, 5, 6))
ROUNDS_IN = (4, 3, 5, 1, 7, 6, 2)
ROUNDS_OUT = (4, 3, 5, 7, 6, 2, 1)
QUERY_TILE = 512
LANES = 128
HEADS_VMEM = 40 * 1024 * 1024
SMALL_VMEM = 8 * 1024 * 1024

BF16 = jnp.bfloat16
F32 = jnp.float32
ROWS_BY_ROWS = (((1,), (1,)), ((), ()))
VMEM = pl.BlockSpec(memory_space=pltpu.VMEM)
SMEM = pl.BlockSpec(memory_space=pltpu.SMEM)


def owner_code(owners):
    return sum((head + 1) << (3 * place) for head, place in enumerate(owners))


def place_and_code():
    place = lax.rem(lax.axis_index("seq"), GROUP)
    odd = lax.rem(lax.axis_index("sec"), 2) == 1
    code = jnp.where(odd, owner_code(OWNERS[1]), owner_code(OWNERS[0])).astype(jnp.int32)
    return place, code


def head_at(code, place):
    return lax.bitwise_and(lax.shift_right_logical(code, 3 * place), 7) - 1


def columns_of(head):
    return pl.ds(pl.multiple_of(head * HS, HS), HS)


def pack_kernel(student_ref, target_ref, *refs):
    slots, sems = in_slot_order(refs, ROUNDS_IN), refs[GROUP]
    place, code = place_and_code()

    def copies(k, head):
        return [
            pltpu.make_async_copy(
                view.at[:, :, columns_of(head)], slots[k].at[pl.ds(3 * i, 3)], sems.at[k, i]
            )
            for i, view in enumerate((student_ref, target_ref))
        ]

    for step in ("start", "wait"):
        for k in ROUNDS_IN + (0,):
            head = head_at(code, lax.bitwise_xor(place, k))

            @pl.when(head >= 0)
            def _():
                for copy in copies(k, head):
                    copy.start() if step == "start" else copy.wait()


def in_slot_order(refs, rounds):
    return [refs[((0,) + rounds).index(k)] for k in range(GROUP)]


def head_kernel(clip_count, extra, lengths_ref, *refs):
    slots = in_slot_order(refs, ROUNDS_IN) + list(refs[GROUP : GROUP + extra])
    refs = refs[GROUP + extra :]
    outs = in_slot_order(refs, ROUNDS_OUT) + list(refs[GROUP : GROUP + extra])
    data, turned, grads, totals_ref = refs[GROUP + extra :]
    place, code = place_and_code()
    rows = slots[0].shape[1]
    scale = 1.0 / math.sqrt(HS)
    to_log2 = scale * math.log2(math.e)
    totals_ref[...] = jnp.zeros_like(totals_ref)
    clip_rows = totals_ref.shape[0]
    outs[0][4 * rows :] = jnp.zeros((2 * clip_rows, HS), BF16)

    def rows_of(slot):
        block = lax.bitwise_xor(place, slot) if slot < GROUP else slot
        return pl.ds(pl.multiple_of(block * rows, rows), rows)

    def clip_pass(blocks, clip, start, length):
        size = blocks * LANES
        first = pl.multiple_of(lax.div(start, LANES) * LANES, LANES)
        window = pl.ds(first, size)
        start = start - first
        key_row = lax.broadcasted_iota(jnp.int32, (LANES, LANES), 0)
        query_column = lax.broadcasted_iota(jnp.int32, (1, size), 1)
        inside = (query_column >= start) & (query_column < start + length)

        def masked(scores):
            parts = [scores[i * LANES : (i + 1) * LANES] for i in range(blocks)]
            for i in sorted({0, blocks - 1}):
                row = key_row + i * LANES
                allowed = (row >= start) & (row < start + length)
                allowed = jnp.concatenate([allowed] * (scores.shape[1] // LANES), axis=1)
                parts[i] = jnp.where(allowed, parts[i], -jnp.inf)
            return jnp.concatenate(parts, axis=0) if blocks > 1 else parts[0]

        def attend(part, turn, mine):
            scores = lax.dot_general(
                data[part + 1, window, :], data[part, mine, :], ROWS_BY_ROWS, preferred_element_type=F32
            )
            scores = masked(scores)
            peak = jnp.max(scores, axis=0, keepdims=True)
            exponent = jnp.exp2((scores - peak) * to_log2)
            inverse = 1.0 / jnp.sum(exponent, axis=0, keepdims=True)
            weights = exponent.astype(BF16)
            out = jnp.dot(turned[turn, :, window], weights, preferred_element_type=F32) * inverse
            return out, exponent, weights, inverse

        dkey = dvalue = total = None
        for begin in range(0, size, QUERY_TILE):
            width = min(QUERY_TILE, size - begin)
            mine = pl.ds(first + begin, width)
            columns = slice(begin, begin + width)
            target, _, _, _ = attend(3, 2, mine)
            student, exponent, weights, inverse = attend(0, 1, mine)
            target = jnp.where(inside[:, columns], target, 0.0)
            diff = jnp.where(inside[:, columns], student - target, 0.0)
            squares = jnp.sum(diff * diff, axis=1, keepdims=True)
            total = squares if total is None else total + squares
            gradient = (diff * inverse).astype(BF16)
            delta = jnp.sum(gradient.astype(F32) * student, axis=0, keepdims=True)
            slope = jnp.dot(data[2, window, :], gradient, preferred_element_type=F32)
            dscores = (exponent * (slope - delta)).astype(BF16)
            dquery = jnp.dot(turned[0, :, window], dscores, preferred_element_type=F32)
            key_part = jnp.dot(dscores, data[0, mine, :], preferred_element_type=F32)
            value_part = lax.dot_general(weights, gradient, ROWS_BY_ROWS, preferred_element_type=F32)
            grads[0, mine, :] += (dquery * scale).T
            grads[3, mine, :] += target.T
            dkey = key_part if dkey is None else dkey + key_part
            dvalue = value_part if dvalue is None else dvalue + value_part
        grads[1, window, :] += dkey * scale
        grads[2, window, :] += dvalue
        clip_iota = lax.broadcasted_iota(jnp.int32, (clip_rows, 1), 0)
        total = jnp.sum(total, axis=0, keepdims=True)
        totals_ref[...] += jnp.where(clip_iota == clip, total, 0.0)

    @pl.when(head_at(code, place) >= 0)
    def _():
        group_start = lax.div(lax.axis_index("seq"), GROUP) * (GROUP * rows)
        for slot in range(GROUP + extra):
            where = rows_of(slot)
            for part in range(6):
                data[part, where, :] = slots[slot][part]
            for turn, part in enumerate((1, 2, 5)):
                turned[turn, :, where] = slots[slot][part].T
        grads[...] = jnp.zeros_like(grads)

        def one_clip(clip, begin):
            length = lengths_ref[clip]
            start = begin - group_start

            @pl.when((start >= 0) & (start < GROUP * rows))
            def _():
                lead = lax.rem(start, LANES)
                blocks = lax.div(lead + length + LANES - 1, LANES)
                for count in range(1, MOST // LANES + 2):

                    @pl.when(blocks == count)
                    def _():
                        clip_pass(count, clip, start, length)

            return begin + length

        lax.fori_loop(0, clip_count, one_clip, jnp.int32(0))
        high = totals_ref[...].astype(BF16)
        low = (totals_ref[...] - high.astype(F32)).astype(BF16)
        for slot in range(GROUP + extra):
            where = rows_of(slot)
            for part in range(4):
                outs[slot][part * rows : (part + 1) * rows] = grads[part, where, :].astype(BF16)
            outs[slot][4 * rows : 4 * rows + clip_rows] = high
            outs[slot][4 * rows + clip_rows :] = low


def sum_kernel(*refs):
    out = refs[-1]
    clip_rows = out.shape[0]
    total = jnp.zeros(out.shape, F32)
    for slot in refs[:-1]:
        start = slot.shape[0] - 2 * clip_rows
        total = total + slot[start : start + clip_rows].astype(F32)
        total = total + slot[start + clip_rows :].astype(F32)
    out[...] = total


def finish_kernel(clip_count, head_count, extra, lengths_ref, mine_ref, other_ref, *refs):
    slots, extras, (grads_ref, target_ref) = in_slot_order(refs, ROUNDS_OUT), refs[GROUP:-2], refs[-2:]
    place, code = place_and_code()
    rows = target_ref.shape[0]
    totals = mine_ref[...] + other_ref[...]
    first = lax.axis_index("seq") * rows
    token = first + lax.broadcasted_iota(jnp.int32, (rows, HS), 0)
    factor = jnp.zeros((rows, HS), F32)
    begin = jnp.int32(0)
    for clip in range(clip_count):
        length = lengths_ref[clip]
        size = length.astype(F32) * (H * HS)
        value = lax.rsqrt(totals[clip : clip + 1, :] / size + EPS)
        factor = jnp.where((token >= begin) & (token < begin + length), value, factor)
        begin = begin + length
    for k in range(GROUP):
        head = head_at(code, lax.bitwise_xor(place, k))

        @pl.when(head >= 0)
        def _():
            cols = columns_of(head)
            for part in range(3):
                block = slots[k][part * rows : (part + 1) * rows].astype(F32)
                grads_ref[part, :, cols] = (block * factor).astype(BF16)
            target_ref[:, cols] = slots[k][3 * rows : 4 * rows]

    for head in range(head_count if extra else 0):
        cols = slice(head * HS, (head + 1) * HS)
        for part in range(3):
            more = extras[head][part * rows : (part + 1) * rows].astype(F32)
            more = (more * factor).astype(BF16)
            grads_ref[part, :, cols] = grads_ref[part, :, cols] + more
        target_ref[:, cols] = target_ref[:, cols] + extras[head][3 * rows : 4 * rows]


def both_axes(sec_count, seq_count, pairs_of):
    pairs = []
    for sec in range(sec_count):
        for start in range(0, seq_count, GROUP):
            for source, target in pairs_of(OWNERS[sec % 2], start):
                if source < seq_count and target < seq_count:
                    pairs.append((sec * seq_count + source, sec * seq_count + target))
    return pairs


def per_device(sec_count, seq_count, student_qkv, target_qkv, clip_lengths):
    rows, _, width = student_qkv.shape
    head_count = width // HS
    clip_count = clip_lengths.shape[0]
    clip_rows = -(-clip_count // 8) * 8
    extra = MOST // rows if seq_count > GROUP else 0
    axes = ("sec", "seq")
    pairs = functools.partial(both_axes, sec_count, seq_count)
    small = pltpu.CompilerParams(vmem_limit_bytes=SMALL_VMEM)

    packed = pl.pallas_call(
        pack_kernel,
        out_shape=[jax.ShapeDtypeStruct((6, rows, HS), BF16)] * GROUP,
        in_specs=[pl.BlockSpec(memory_space=pltpu.HBM)] * 2,
        out_specs=[VMEM] * GROUP,
        scratch_shapes=[pltpu.SemaphoreType.DMA((GROUP, 2))],
        compiler_params=small,
        name="pack",
    )(
        pltpu.with_memory_space_constraint(jnp.transpose(student_qkv, (1, 0, 2)), pltpu.HBM),
        pltpu.with_memory_space_constraint(jnp.transpose(target_qkv, (1, 0, 2)), pltpu.HBM),
    )

    gathered = [packed[0]]
    for k, mine in zip(ROUNDS_IN, packed[1:]):
        gathered.append(
            lax.ppermute(
                mine, axes, pairs(lambda owners, start: [(start + (d ^ k), start + d) for d in owners])
            )
        )
    for block in range(extra):
        pieces = []
        for head in range(head_count):
            cols = slice(head * HS, (head + 1) * HS)
            piece = jnp.concatenate([student_qkv[:, :, cols], target_qkv[:, :, cols]], axis=1)
            pieces.append(
                lax.ppermute(
                    jnp.transpose(piece, (1, 0, 2)),
                    axes,
                    pairs(lambda owners, start: [(start + GROUP + block, start + owners[head])]),
                )
            )
        gathered.append(sum(pieces[1:], pieces[0]))

    tokens = (GROUP + extra) * rows
    payload = jax.ShapeDtypeStruct((4 * rows + 2 * clip_rows, HS), BF16)
    results = pl.pallas_call(
        functools.partial(head_kernel, clip_count, extra),
        out_shape=[payload] * (GROUP + extra),
        in_specs=[SMEM] + [VMEM] * (GROUP + extra),
        out_specs=[VMEM] * (GROUP + extra),
        scratch_shapes=[
            pltpu.VMEM((6, tokens, HS), BF16),
            pltpu.VMEM((3, HS, tokens), BF16),
            pltpu.VMEM((4, tokens, HS), F32),
            pltpu.VMEM((clip_rows, HS), F32),
        ],
        compiler_params=pltpu.CompilerParams(vmem_limit_bytes=HEADS_VMEM),
        name="heads",
    )(clip_lengths, *gathered)

    returned = [results[0]]
    for k, mine in zip(ROUNDS_OUT, results[1:]):
        returned.append(
            lax.ppermute(
                mine, axes, pairs(lambda owners, start: [(start + d, start + (d ^ k)) for d in owners])
            )
        )
    extras = []
    for head in range(head_count if extra else 0):
        pieces = [
            lax.ppermute(
                results[GROUP + block],
                axes,
                pairs(lambda owners, start: [(start + owners[head], start + GROUP + block)]),
            )
            for block in range(extra)
        ]
        extras.append(sum(pieces[1:], pieces[0]))
    totals = pl.pallas_call(
        sum_kernel,
        out_shape=jax.ShapeDtypeStruct((clip_rows, HS), F32),
        in_specs=[VMEM] * GROUP,
        out_specs=VMEM,
        compiler_params=small,
        name="totals",
    )(*returned)

    def over(totals, axis, count, step):
        return lax.ppermute(totals, axis, [(s, s ^ step) for s in range(count)])

    step = GROUP
    while step < seq_count:
        totals = totals + over(totals, "seq", seq_count, step)
        step *= 2
    step = 1
    while 2 * step < sec_count:
        totals = totals + over(totals, "sec", sec_count, step)
        step *= 2

    grads, target_out = pl.pallas_call(
        functools.partial(finish_kernel, clip_count, head_count, extra),
        out_shape=[
            jax.ShapeDtypeStruct((3, rows, width), BF16),
            jax.ShapeDtypeStruct((rows, width), BF16),
        ],
        in_specs=[SMEM] + [VMEM] * (2 + GROUP + len(extras)),
        out_specs=[VMEM] * 2,
        compiler_params=small,
        name="finish",
    )(clip_lengths, totals, over(totals, "sec", sec_count, step), *returned, *extras)
    return jnp.transpose(grads, (1, 0, 2)), target_out


def solution(mesh):
    return jax.shard_map(
        functools.partial(per_device, mesh.shape["sec"], mesh.shape["seq"]),
        mesh=mesh,
        in_specs=(P("seq", None, "sec"), P("seq", None, "sec"), P()),
        out_specs=(P("seq", None, "sec"), P("seq", "sec")),
        check_vma=False,
    )
```

```python
import functools
import math

import jax
import jax.numpy as jnp
from jax import lax
from jax.experimental import pallas as pl
from jax.experimental.pallas import tpu as pltpu
from jax.sharding import PartitionSpec as P

H = 20
HS = 128
MOST = 384
EPS = 1e-05

GROUP = 8
OWNERS = ((0, 2, 4, 5, 7), (1, 2, 3, 5, 6))
ROUNDS_IN = (4, 3, 5, 1, 7, 6, 2)
ROUNDS_OUT = (7, 3, 5, 4, 2, 6, 1)
QUERY_TILE = 512
LANES = 128
HEADS_VMEM = 40 * 1024 * 1024
SMALL_VMEM = 8 * 1024 * 1024

BF16 = jnp.bfloat16
F32 = jnp.float32
ROWS_BY_ROWS = (((1,), (1,)), ((), ()))
VMEM = pl.BlockSpec(memory_space=pltpu.VMEM)
SMEM = pl.BlockSpec(memory_space=pltpu.SMEM)


def owner_code(owners):
    return sum((head + 1) << (3 * place) for head, place in enumerate(owners))


def place_and_code():
    place = lax.rem(lax.axis_index("seq"), GROUP)
    odd = lax.rem(lax.axis_index("sec"), 2) == 1
    code = jnp.where(odd, owner_code(OWNERS[1]), owner_code(OWNERS[0])).astype(jnp.int32)
    return place, code


def head_at(code, place):
    return lax.bitwise_and(lax.shift_right_logical(code, 3 * place), 7) - 1


def columns_of(head):
    return pl.ds(pl.multiple_of(head * HS, HS), HS)


def pack_kernel(student_ref, target_ref, *refs):
    slots, sems = in_slot_order(refs, ROUNDS_IN), refs[GROUP]
    place, code = place_and_code()

    def copies(k, head):
        return [
            pltpu.make_async_copy(
                view.at[:, :, columns_of(head)], slots[k].at[pl.ds(3 * i, 3)], sems.at[k, i]
            )
            for i, view in enumerate((student_ref, target_ref))
        ]

    for step in ("start", "wait"):
        for k in ROUNDS_IN + (0,):
            head = head_at(code, lax.bitwise_xor(place, k))

            @pl.when(head >= 0)
            def _():
                for copy in copies(k, head):
                    copy.start() if step == "start" else copy.wait()


def in_slot_order(refs, rounds):
    return [refs[((0,) + rounds).index(k)] for k in range(GROUP)]


def head_kernel(clip_count, extra, lengths_ref, *refs):
    slots = in_slot_order(refs, ROUNDS_IN) + list(refs[GROUP : GROUP + extra])
    refs = refs[GROUP + extra :]
    outs = in_slot_order(refs, ROUNDS_OUT) + list(refs[GROUP : GROUP + extra])
    data, turned, grads, totals_ref = refs[GROUP + extra :]
    place, code = place_and_code()
    rows = slots[0].shape[1]
    scale = 1.0 / math.sqrt(HS)
    to_log2 = scale * math.log2(math.e)
    totals_ref[...] = jnp.zeros_like(totals_ref)
    clip_rows = totals_ref.shape[0]
    outs[0][4 * rows :] = jnp.zeros((2 * clip_rows, HS), BF16)

    def rows_of(slot):
        block = lax.bitwise_xor(place, slot) if slot < GROUP else slot
        return pl.ds(pl.multiple_of(block * rows, rows), rows)

    def clip_pass(blocks, clip, start, length):
        size = blocks * LANES
        first = pl.multiple_of(lax.div(start, LANES) * LANES, LANES)
        window = pl.ds(first, size)
        start = start - first
        query_column = lax.broadcasted_iota(jnp.int32, (1, size), 1)
        inside = (query_column >= start) & (query_column < start + length)

        def masked(scores, axis):
            parts = jnp.split(scores, blocks, axis=axis)
            for i in sorted({0, blocks - 1}):
                key = lax.broadcasted_iota(jnp.int32, parts[i].shape, axis) + i * LANES
                parts[i] = jnp.where((key >= start) & (key < start + length), parts[i], -jnp.inf)
            return jnp.concatenate(parts, axis=axis)

        def softmax(scores, axis):
            peak = jnp.max(scores, axis=axis, keepdims=True)
            exponent = jnp.exp2((scores - peak) * to_log2)
            return exponent, 1.0 / jnp.sum(exponent, axis=axis, keepdims=True)

        def product(a, b):
            return lax.dot_general(a, b, ROWS_BY_ROWS, preferred_element_type=F32)

        dkey = dvalue = total = None
        for begin in range(0, size, QUERY_TILE):
            width = min(QUERY_TILE, size - begin)
            mine = pl.ds(first + begin, width)
            columns = slice(begin, begin + width)
            exponent, inverse = softmax(masked(product(data[3, mine, :], data[4, window, :]), 1), 1)
            target = jnp.dot(exponent.astype(BF16), data[5, window, :], preferred_element_type=F32)
            target = target * inverse
            exponent, inverse = softmax(masked(product(data[1, window, :], data[0, mine, :]), 0), 0)
            weights = exponent.astype(BF16)
            student = jnp.dot(turned[1, :, window], weights, preferred_element_type=F32) * inverse
            diff = jnp.where(inside[:, columns], student - target.T, 0.0)
            squares = jnp.sum(diff * diff, axis=1, keepdims=True)
            total = squares if total is None else total + squares
            gradient = (diff * inverse).astype(BF16)
            delta = jnp.sum(gradient.astype(F32) * student, axis=0, keepdims=True)
            slope = jnp.dot(data[2, window, :], gradient, preferred_element_type=F32)
            dscores = (exponent * (slope - delta)).astype(BF16)
            dquery = jnp.dot(turned[0, :, window], dscores, preferred_element_type=F32)
            key_part = jnp.dot(dscores, data[0, mine, :], preferred_element_type=F32)
            value_part = product(weights, gradient)
            grads[0, mine, :] += (dquery * scale).T
            query = lax.broadcasted_iota(jnp.int32, (width, HS), 0) + begin
            grads[3, mine, :] += jnp.where((query >= start) & (query < start + length), target, 0.0)
            dkey = key_part if dkey is None else dkey + key_part
            dvalue = value_part if dvalue is None else dvalue + value_part
        grads[1, window, :] += dkey * scale
        grads[2, window, :] += dvalue
        clip_iota = lax.broadcasted_iota(jnp.int32, (clip_rows, 1), 0)
        total = jnp.sum(total, axis=0, keepdims=True)
        totals_ref[...] += jnp.where(clip_iota == clip, total, 0.0)

    @pl.when(head_at(code, place) >= 0)
    def _():
        group_start = lax.div(lax.axis_index("seq"), GROUP) * (GROUP * rows)
        for slot in range(GROUP + extra):
            where = rows_of(slot)
            for part in range(6):
                data[part, where, :] = slots[slot][part]
            for turn, part in enumerate((1, 2)):
                turned[turn, :, where] = slots[slot][part].T
        grads[...] = jnp.zeros_like(grads)

        def one_clip(clip, begin):
            length = lengths_ref[clip]
            start = begin - group_start

            @pl.when((start >= 0) & (start < GROUP * rows))
            def _():
                lead = lax.rem(start, LANES)
                blocks = lax.div(lead + length + LANES - 1, LANES)
                for count in range(1, MOST // LANES + 2):

                    @pl.when(blocks == count)
                    def _():
                        clip_pass(count, clip, start, length)

            return begin + length

        lax.fori_loop(0, clip_count, one_clip, jnp.int32(0))
        high = totals_ref[...].astype(BF16)
        low = (totals_ref[...] - high.astype(F32)).astype(BF16)
        for slot in range(GROUP + extra):
            where = rows_of(slot)
            for part in range(4):
                outs[slot][part * rows : (part + 1) * rows] = grads[part, where, :].astype(BF16)
            outs[slot][4 * rows : 4 * rows + clip_rows] = high
            outs[slot][4 * rows + clip_rows :] = low


def sum_kernel(*refs):
    out = refs[-1]
    clip_rows = out.shape[0]
    total = jnp.zeros(out.shape, F32)
    for slot in refs[:-1]:
        start = slot.shape[0] - 2 * clip_rows
        total = total + slot[start : start + clip_rows].astype(F32)
        total = total + slot[start + clip_rows :].astype(F32)
    out[...] = total


def finish_kernel(clip_count, head_count, extra, sec_count, lengths_ref, *refs):
    sums, refs = refs[:sec_count], refs[sec_count:]
    slots, extras = in_slot_order(refs, ROUNDS_OUT), refs[GROUP:-5]
    grads_out, target_out, grads_ref, target_ref, sems = refs[-5:]
    place, code = place_and_code()
    rows = target_ref.shape[0]
    totals = sum((ref[...] for ref in sums[1:]), sums[0][...])
    first = lax.axis_index("seq") * rows
    token = first + lax.broadcasted_iota(jnp.int32, (rows, HS), 0)
    factor = jnp.zeros((rows, HS), F32)
    begin = jnp.int32(0)
    for clip in range(clip_count):
        length = lengths_ref[clip]
        size = length.astype(F32) * (H * HS)
        value = lax.rsqrt(totals[clip : clip + 1, :] / size + EPS)
        factor = jnp.where((token >= begin) & (token < begin + length), value, factor)
        begin = begin + length
    def for_heads(visit):
        for k in range(GROUP):
            head = head_at(code, lax.bitwise_xor(place, k))
            pl.when(head >= 0)(functools.partial(visit, k, columns_of(head)))

    def copies(k, cols):
        return (
            pltpu.make_async_copy(
                grads_ref.at[:, :, cols], grads_out.at[:, :, cols], sems.at[k, 0]
            ),
            pltpu.make_async_copy(target_ref.at[:, cols], target_out.at[:, cols], sems.at[k, 1]),
        )

    def start(k, cols):
        for copy in copies(k, cols):
            copy.start()

    def wait(k, cols):
        for copy in copies(k, cols):
            copy.wait()

    def scale(k, cols):
        target_ref[:, cols] = slots[k][3 * rows : 4 * rows]
        for part in range(3):
            block = slots[k][part * rows : (part + 1) * rows].astype(F32)
            grads_ref[part, :, cols] = (block * factor).astype(BF16)
        if not extra:
            start(k, cols)

    for_heads(scale)
    for head in range(head_count if extra else 0):
        cols = slice(head * HS, (head + 1) * HS)
        for part in range(3):
            more = extras[head][part * rows : (part + 1) * rows].astype(F32)
            more = (more * factor).astype(BF16)
            grads_ref[part, :, cols] = grads_ref[part, :, cols] + more
        target_ref[:, cols] = target_ref[:, cols] + extras[head][3 * rows : 4 * rows]
    if extra:
        for_heads(start)
    for_heads(wait)


def both_axes(sec_count, seq_count, pairs_of):
    pairs = []
    for sec in range(sec_count):
        for start in range(0, seq_count, GROUP):
            for source, target in pairs_of(OWNERS[sec % 2], start):
                if source < seq_count and target < seq_count:
                    pairs.append((sec * seq_count + source, sec * seq_count + target))
    return pairs


def per_device(sec_count, seq_count, student_qkv, target_qkv, clip_lengths):
    rows, _, width = student_qkv.shape
    head_count = width // HS
    clip_count = clip_lengths.shape[0]
    clip_rows = -(-clip_count // 8) * 8
    extra = MOST // rows if seq_count > GROUP else 0
    axes = ("sec", "seq")
    pairs = functools.partial(both_axes, sec_count, seq_count)
    small = pltpu.CompilerParams(vmem_limit_bytes=SMALL_VMEM)

    packed = pl.pallas_call(
        pack_kernel,
        out_shape=[jax.ShapeDtypeStruct((6, rows, HS), BF16)] * GROUP,
        in_specs=[pl.BlockSpec(memory_space=pltpu.HBM)] * 2,
        out_specs=[VMEM] * GROUP,
        scratch_shapes=[pltpu.SemaphoreType.DMA((GROUP, 2))],
        compiler_params=small,
        name="pack",
    )(
        pltpu.with_memory_space_constraint(jnp.transpose(student_qkv, (1, 0, 2)), pltpu.HBM),
        pltpu.with_memory_space_constraint(jnp.transpose(target_qkv, (1, 0, 2)), pltpu.HBM),
    )

    gathered = [packed[0]]
    for k, mine in zip(ROUNDS_IN, packed[1:]):
        gathered.append(
            lax.ppermute(
                mine, axes, pairs(lambda owners, start: [(start + (d ^ k), start + d) for d in owners])
            )
        )
    for block in range(extra):
        pieces = []
        for head in range(head_count):
            cols = slice(head * HS, (head + 1) * HS)
            piece = jnp.concatenate([student_qkv[:, :, cols], target_qkv[:, :, cols]], axis=1)
            pieces.append(
                lax.ppermute(
                    jnp.transpose(piece, (1, 0, 2)),
                    axes,
                    pairs(lambda owners, start: [(start + GROUP + block, start + owners[head])]),
                )
            )
        gathered.append(sum(pieces[1:], pieces[0]))

    tokens = (GROUP + extra) * rows
    payload = jax.ShapeDtypeStruct((4 * rows + 2 * clip_rows, HS), BF16)
    results = pl.pallas_call(
        functools.partial(head_kernel, clip_count, extra),
        out_shape=[payload] * (GROUP + extra),
        in_specs=[SMEM] + [VMEM] * (GROUP + extra),
        out_specs=[VMEM] * (GROUP + extra),
        scratch_shapes=[
            pltpu.VMEM((6, tokens, HS), BF16),
            pltpu.VMEM((2, HS, tokens), BF16),
            pltpu.VMEM((4, tokens, HS), F32),
            pltpu.VMEM((clip_rows, HS), F32),
        ],
        compiler_params=pltpu.CompilerParams(vmem_limit_bytes=HEADS_VMEM),
        name="heads",
    )(clip_lengths, *gathered)

    returned = [results[0]]
    for k, mine in zip(ROUNDS_OUT, results[1:]):
        returned.append(
            lax.ppermute(
                mine, axes, pairs(lambda owners, start: [(start + d, start + (d ^ k)) for d in owners])
            )
        )
    extras = []
    for head in range(head_count if extra else 0):
        pieces = [
            lax.ppermute(
                results[GROUP + block],
                axes,
                pairs(lambda owners, start: [(start + owners[head], start + GROUP + block)]),
            )
            for block in range(extra)
        ]
        extras.append(sum(pieces[1:], pieces[0]))
    totals = pl.pallas_call(
        sum_kernel,
        out_shape=jax.ShapeDtypeStruct((clip_rows, HS), F32),
        in_specs=[VMEM] * GROUP,
        out_specs=VMEM,
        compiler_params=small,
        name="totals",
    )(*returned)

    def over(totals, axis, count, step):
        return lax.ppermute(totals, axis, [(s, s ^ step) for s in range(count)])

    step = GROUP
    while step < seq_count:
        totals = totals + over(totals, "seq", seq_count, step)
        step *= 2
    others = [over(totals, "sec", sec_count, step) for step in range(1, sec_count)]

    grads, target_out = pl.pallas_call(
        functools.partial(finish_kernel, clip_count, head_count, extra, sec_count),
        out_shape=[
            jax.ShapeDtypeStruct((3, rows, width), BF16),
            jax.ShapeDtypeStruct((rows, width), BF16),
        ],
        in_specs=[SMEM] + [VMEM] * (sec_count + GROUP + len(extras)),
        out_specs=[pl.BlockSpec(memory_space=pltpu.HBM)] * 2,
        scratch_shapes=[
            pltpu.VMEM((3, rows, width), BF16),
            pltpu.VMEM((rows, width), BF16),
            pltpu.SemaphoreType.DMA((GROUP, 2)),
        ],
        compiler_params=small,
        name="finish",
    )(clip_lengths, totals, *others, *returned, *extras)
    return jnp.transpose(grads, (1, 0, 2)), target_out


def solution(mesh):
    return jax.shard_map(
        functools.partial(per_device, mesh.shape["sec"], mesh.shape["seq"]),
        mesh=mesh,
        in_specs=(P("seq", None, "sec"), P("seq", None, "sec"), P()),
        out_specs=(P("seq", None, "sec"), P("seq", "sec")),
        check_vma=False,
    )
```

```python
import functools
import math

import jax
import jax.numpy as jnp
from jax import lax
from jax.experimental import pallas as pl
from jax.experimental.pallas import tpu as pltpu
from jax.sharding import PartitionSpec as P

H = 20
HS = 128
MOST = 384
EPS = 1e-05

GROUP = 8
OWNERS = ((0, 2, 4, 5, 7), (1, 2, 3, 5, 6))
ROUNDS_IN = (4, 3, 5, 1, 7, 6, 2)
ROUNDS_OUT = (7, 3, 5, 4, 2, 6, 1)
QUERY_TILE = 512
LANES = 128
HEADS_VMEM = 40 * 1024 * 1024
SMALL_VMEM = 8 * 1024 * 1024

BF16 = jnp.bfloat16
F32 = jnp.float32
ROWS_BY_ROWS = (((1,), (1,)), ((), ()))
VMEM = pl.BlockSpec(memory_space=pltpu.VMEM)
SMEM = pl.BlockSpec(memory_space=pltpu.SMEM)


def owner_code(owners):
    return sum((head + 1) << (3 * place) for head, place in enumerate(owners))


def place_and_code():
    place = lax.rem(lax.axis_index("seq"), GROUP)
    odd = lax.rem(lax.axis_index("sec"), 2) == 1
    code = jnp.where(odd, owner_code(OWNERS[1]), owner_code(OWNERS[0])).astype(jnp.int32)
    return place, code


def head_at(code, place):
    return lax.bitwise_and(lax.shift_right_logical(code, 3 * place), 7) - 1


def columns_of(head):
    return pl.ds(pl.multiple_of(head * HS, HS), HS)


def pack_kernel(student_ref, target_ref, *refs):
    slots, sems = in_slot_order(refs, ROUNDS_IN), refs[GROUP]
    place, code = place_and_code()

    def copies(k, head):
        return [
            pltpu.make_async_copy(
                view.at[:, :, columns_of(head)], slots[k].at[pl.ds(3 * i, 3)], sems.at[k, i]
            )
            for i, view in enumerate((student_ref, target_ref))
        ]

    for step in ("start", "wait"):
        for k in ROUNDS_IN + (0,):
            head = head_at(code, lax.bitwise_xor(place, k))

            @pl.when(head >= 0)
            def _():
                for copy in copies(k, head):
                    copy.start() if step == "start" else copy.wait()


def in_slot_order(refs, rounds):
    return [refs[((0,) + rounds).index(k)] for k in range(GROUP)]


def head_kernel(clip_count, extra, lengths_ref, *refs):
    slots = in_slot_order(refs, ROUNDS_IN) + list(refs[GROUP : GROUP + extra])
    refs = refs[GROUP + extra :]
    outs = in_slot_order(refs, ROUNDS_OUT) + list(refs[GROUP : GROUP + extra])
    data, turned, grads, totals_ref = refs[GROUP + extra :]
    place, code = place_and_code()
    rows = slots[0].shape[1]
    scale = 1.0 / math.sqrt(HS)
    to_log2 = scale * math.log2(math.e)
    totals_ref[...] = jnp.zeros_like(totals_ref)
    clip_rows = totals_ref.shape[0]
    outs[0][4 * rows :] = jnp.zeros((2 * clip_rows, HS), BF16)

    def rows_of(slot):
        block = lax.bitwise_xor(place, slot) if slot < GROUP else slot
        return pl.ds(pl.multiple_of(block * rows, rows), rows)

    def clip_pass(blocks, clip, start, length):
        size = blocks * LANES
        first = pl.multiple_of(lax.div(start, LANES) * LANES, LANES)
        window = pl.ds(first, size)
        start = start - first
        query_column = lax.broadcasted_iota(jnp.int32, (1, size), 1)
        inside = (query_column >= start) & (query_column < start + length)

        def masked(scores, axis):
            parts = jnp.split(scores, blocks, axis=axis)
            for i in sorted({0, blocks - 1}):
                key = lax.broadcasted_iota(jnp.int32, parts[i].shape, axis) + i * LANES
                parts[i] = jnp.where((key >= start) & (key < start + length), parts[i], -jnp.inf)
            return jnp.concatenate(parts, axis=axis)

        def powers(scores, axis):
            peak = jnp.max(scores, axis=axis, keepdims=True)
            return jnp.exp2((scores - peak) * to_log2)

        def product(a, b):
            return lax.dot_general(a, b, ROWS_BY_ROWS, preferred_element_type=F32)

        dkey = dvalue = total = None
        for begin in range(0, size, QUERY_TILE):
            width = min(QUERY_TILE, size - begin)
            mine = pl.ds(first + begin, width)
            columns = slice(begin, begin + width)
            exponent = powers(masked(product(data[3, mine, :], data[4, window, :]), 1), 1)
            values = jnp.concatenate([data[5, window, :], jnp.ones((size, HS), BF16)], axis=1)
            both = jnp.dot(exponent.astype(BF16), values, preferred_element_type=F32)
            target = both[:, :HS] * (1.0 / both[:, HS:])
            exponent = powers(masked(product(data[1, window, :], data[0, mine, :]), 0), 0)
            weights = exponent.astype(BF16)
            inverse = 1.0 / jnp.sum(exponent, axis=0, keepdims=True)
            student = jnp.dot(turned[1, :, window], weights, preferred_element_type=F32) * inverse
            diff = jnp.where(inside[:, columns], student - target.T, 0.0)
            squares = jnp.sum(diff * diff, axis=1, keepdims=True)
            total = squares if total is None else total + squares
            gradient = (diff * inverse).astype(BF16)
            delta = jnp.sum(gradient.astype(F32) * student, axis=0, keepdims=True)
            slope = jnp.dot(data[2, window, :], gradient, preferred_element_type=F32)
            dscores = (exponent * (slope - delta)).astype(BF16)
            dquery = jnp.dot(turned[0, :, window], dscores, preferred_element_type=F32)
            key_part = jnp.dot(dscores, data[0, mine, :], preferred_element_type=F32)
            value_part = product(weights, gradient)
            grads[0, mine, :] += (dquery * scale).T
            query = lax.broadcasted_iota(jnp.int32, (width, HS), 0) + begin
            grads[3, mine, :] += jnp.where((query >= start) & (query < start + length), target, 0.0)
            dkey = key_part if dkey is None else dkey + key_part
            dvalue = value_part if dvalue is None else dvalue + value_part
        grads[1, window, :] += dkey * scale
        grads[2, window, :] += dvalue
        clip_iota = lax.broadcasted_iota(jnp.int32, (clip_rows, 1), 0)
        total = jnp.sum(total, axis=0, keepdims=True)
        totals_ref[...] += jnp.where(clip_iota == clip, total, 0.0)

    @pl.when(head_at(code, place) >= 0)
    def _():
        group_start = lax.div(lax.axis_index("seq"), GROUP) * (GROUP * rows)
        for slot in range(GROUP + extra):
            where = rows_of(slot)
            for part in range(6):
                data[part, where, :] = slots[slot][part]
            for turn, part in enumerate((1, 2)):
                turned[turn, :, where] = slots[slot][part].T
        grads[...] = jnp.zeros_like(grads)

        def one_clip(clip, begin):
            length = lengths_ref[clip]
            start = begin - group_start

            @pl.when((start >= 0) & (start < GROUP * rows))
            def _():
                lead = lax.rem(start, LANES)
                blocks = lax.div(lead + length + LANES - 1, LANES)
                for count in range(1, MOST // LANES + 2):

                    @pl.when(blocks == count)
                    def _():
                        clip_pass(count, clip, start, length)

            return begin + length

        lax.fori_loop(0, clip_count, one_clip, jnp.int32(0))
        high = totals_ref[...].astype(BF16)
        low = (totals_ref[...] - high.astype(F32)).astype(BF16)
        for slot in range(GROUP + extra):
            where = rows_of(slot)
            for part in range(4):
                outs[slot][part * rows : (part + 1) * rows] = grads[part, where, :].astype(BF16)
            outs[slot][4 * rows : 4 * rows + clip_rows] = high
            outs[slot][4 * rows + clip_rows :] = low


def sum_kernel(*refs):
    out = refs[-1]
    clip_rows = out.shape[0]
    total = jnp.zeros(out.shape, F32)
    for slot in refs[:-1]:
        start = slot.shape[0] - 2 * clip_rows
        total = total + slot[start : start + clip_rows].astype(F32)
        total = total + slot[start + clip_rows :].astype(F32)
    out[...] = total


def finish_kernel(clip_count, head_count, extra, sec_count, lengths_ref, *refs):
    sums, refs = refs[:sec_count], refs[sec_count:]
    slots, extras = in_slot_order(refs, ROUNDS_OUT), refs[GROUP:-5]
    grads_out, target_out, grads_ref, target_ref, sems = refs[-5:]
    place, code = place_and_code()
    rows = target_ref.shape[0]
    totals = sum((ref[...] for ref in sums[1:]), sums[0][...])
    first = lax.axis_index("seq") * rows
    token = first + lax.broadcasted_iota(jnp.int32, (rows, HS), 0)
    factor = jnp.zeros((rows, HS), F32)
    begin = jnp.int32(0)
    for clip in range(clip_count):
        length = lengths_ref[clip]
        size = length.astype(F32) * (H * HS)
        value = lax.rsqrt(totals[clip : clip + 1, :] / size + EPS)
        factor = jnp.where((token >= begin) & (token < begin + length), value, factor)
        begin = begin + length
    def for_heads(visit):
        for k in range(GROUP):
            head = head_at(code, lax.bitwise_xor(place, k))
            pl.when(head >= 0)(functools.partial(visit, k, columns_of(head)))

    def copies(k, cols):
        return (
            pltpu.make_async_copy(
                grads_ref.at[:, :, cols], grads_out.at[:, :, cols], sems.at[k, 0]
            ),
            pltpu.make_async_copy(target_ref.at[:, cols], target_out.at[:, cols], sems.at[k, 1]),
        )

    def start(k, cols):
        for copy in copies(k, cols):
            copy.start()

    def wait(k, cols):
        for copy in copies(k, cols):
            copy.wait()

    def scale(k, cols):
        target_ref[:, cols] = slots[k][3 * rows : 4 * rows]
        for part in range(3):
            block = slots[k][part * rows : (part + 1) * rows].astype(F32)
            grads_ref[part, :, cols] = (block * factor).astype(BF16)
        if not extra:
            start(k, cols)

    for_heads(scale)
    for head in range(head_count if extra else 0):
        cols = slice(head * HS, (head + 1) * HS)
        for part in range(3):
            more = extras[head][part * rows : (part + 1) * rows].astype(F32)
            more = (more * factor).astype(BF16)
            grads_ref[part, :, cols] = grads_ref[part, :, cols] + more
        target_ref[:, cols] = target_ref[:, cols] + extras[head][3 * rows : 4 * rows]
    if extra:
        for_heads(start)
    for_heads(wait)


def both_axes(sec_count, seq_count, pairs_of):
    pairs = []
    for sec in range(sec_count):
        for start in range(0, seq_count, GROUP):
            for source, target in pairs_of(OWNERS[sec % 2], start):
                if source < seq_count and target < seq_count:
                    pairs.append((sec * seq_count + source, sec * seq_count + target))
    return pairs


def per_device(sec_count, seq_count, student_qkv, target_qkv, clip_lengths):
    rows, _, width = student_qkv.shape
    head_count = width // HS
    clip_count = clip_lengths.shape[0]
    clip_rows = -(-clip_count // 8) * 8
    extra = MOST // rows if seq_count > GROUP else 0
    axes = ("sec", "seq")
    pairs = functools.partial(both_axes, sec_count, seq_count)
    small = pltpu.CompilerParams(vmem_limit_bytes=SMALL_VMEM)

    packed = pl.pallas_call(
        pack_kernel,
        out_shape=[jax.ShapeDtypeStruct((6, rows, HS), BF16)] * GROUP,
        in_specs=[pl.BlockSpec(memory_space=pltpu.HBM)] * 2,
        out_specs=[VMEM] * GROUP,
        scratch_shapes=[pltpu.SemaphoreType.DMA((GROUP, 2))],
        compiler_params=small,
        name="pack",
    )(
        pltpu.with_memory_space_constraint(jnp.transpose(student_qkv, (1, 0, 2)), pltpu.HBM),
        pltpu.with_memory_space_constraint(jnp.transpose(target_qkv, (1, 0, 2)), pltpu.HBM),
    )

    gathered = [packed[0]]
    for k, mine in zip(ROUNDS_IN, packed[1:]):
        gathered.append(
            lax.ppermute(
                mine, axes, pairs(lambda owners, start: [(start + (d ^ k), start + d) for d in owners])
            )
        )
    for block in range(extra):
        pieces = []
        for head in range(head_count):
            cols = slice(head * HS, (head + 1) * HS)
            piece = jnp.concatenate([student_qkv[:, :, cols], target_qkv[:, :, cols]], axis=1)
            pieces.append(
                lax.ppermute(
                    jnp.transpose(piece, (1, 0, 2)),
                    axes,
                    pairs(lambda owners, start: [(start + GROUP + block, start + owners[head])]),
                )
            )
        gathered.append(sum(pieces[1:], pieces[0]))

    tokens = (GROUP + extra) * rows
    payload = jax.ShapeDtypeStruct((4 * rows + 2 * clip_rows, HS), BF16)
    results = pl.pallas_call(
        functools.partial(head_kernel, clip_count, extra),
        out_shape=[payload] * (GROUP + extra),
        in_specs=[SMEM] + [VMEM] * (GROUP + extra),
        out_specs=[VMEM] * (GROUP + extra),
        scratch_shapes=[
            pltpu.VMEM((6, tokens, HS), BF16),
            pltpu.VMEM((2, HS, tokens), BF16),
            pltpu.VMEM((4, tokens, HS), F32),
            pltpu.VMEM((clip_rows, HS), F32),
        ],
        compiler_params=pltpu.CompilerParams(vmem_limit_bytes=HEADS_VMEM),
        name="heads",
    )(clip_lengths, *gathered)

    returned = [results[0]]
    for k, mine in zip(ROUNDS_OUT, results[1:]):
        returned.append(
            lax.ppermute(
                mine, axes, pairs(lambda owners, start: [(start + d, start + (d ^ k)) for d in owners])
            )
        )
    extras = []
    for head in range(head_count if extra else 0):
        pieces = [
            lax.ppermute(
                results[GROUP + block],
                axes,
                pairs(lambda owners, start: [(start + owners[head], start + GROUP + block)]),
            )
            for block in range(extra)
        ]
        extras.append(sum(pieces[1:], pieces[0]))
    totals = pl.pallas_call(
        sum_kernel,
        out_shape=jax.ShapeDtypeStruct((clip_rows, HS), F32),
        in_specs=[VMEM] * GROUP,
        out_specs=VMEM,
        compiler_params=small,
        name="totals",
    )(*returned)

    def over(totals, axis, count, step):
        return lax.ppermute(totals, axis, [(s, s ^ step) for s in range(count)])

    step = GROUP
    while step < seq_count:
        totals = totals + over(totals, "seq", seq_count, step)
        step *= 2
    others = [over(totals, "sec", sec_count, step) for step in range(1, sec_count)]

    grads, target_out = pl.pallas_call(
        functools.partial(finish_kernel, clip_count, head_count, extra, sec_count),
        out_shape=[
            jax.ShapeDtypeStruct((3, rows, width), BF16),
            jax.ShapeDtypeStruct((rows, width), BF16),
        ],
        in_specs=[SMEM] + [VMEM] * (sec_count + GROUP + len(extras)),
        out_specs=[pl.BlockSpec(memory_space=pltpu.HBM)] * 2,
        scratch_shapes=[
            pltpu.VMEM((3, rows, width), BF16),
            pltpu.VMEM((rows, width), BF16),
            pltpu.SemaphoreType.DMA((GROUP, 2)),
        ],
        compiler_params=small,
        name="finish",
    )(clip_lengths, totals, *others, *returned, *extras)
    return jnp.transpose(grads, (1, 0, 2)), target_out


def solution(mesh):
    return jax.shard_map(
        functools.partial(per_device, mesh.shape["sec"], mesh.shape["seq"]),
        mesh=mesh,
        in_specs=(P("seq", None, "sec"), P("seq", None, "sec"), P()),
        out_specs=(P("seq", None, "sec"), P("seq", "sec")),
        check_vma=False,
    )
```

```python
import functools
import math

import jax
import jax.numpy as jnp
from jax import lax
from jax.experimental import pallas as pl
from jax.experimental.pallas import tpu as pltpu
from jax.sharding import PartitionSpec as P

H = 20
HS = 128
MOST = 384
EPS = 1e-05

GROUP = 8
OWNERS = ((0, 2, 4, 5, 7), (1, 2, 3, 5, 6))
ROUNDS_IN = (4, 3, 5, 1, 7, 6, 2)
ROUNDS_OUT = (7, 3, 5, 4, 2, 6, 1)
QUERY_TILE = 512
LANES = 128
HEADS_VMEM = 40 * 1024 * 1024
SMALL_VMEM = 8 * 1024 * 1024

BF16 = jnp.bfloat16
F32 = jnp.float32
ROWS_BY_ROWS = (((1,), (1,)), ((), ()))
VMEM = pl.BlockSpec(memory_space=pltpu.VMEM)
SMEM = pl.BlockSpec(memory_space=pltpu.SMEM)


def owner_code(owners):
    return sum((head + 1) << (3 * place) for head, place in enumerate(owners))


def place_and_code():
    place = lax.rem(lax.axis_index("seq"), GROUP)
    odd = lax.rem(lax.axis_index("sec"), 2) == 1
    code = jnp.where(odd, owner_code(OWNERS[1]), owner_code(OWNERS[0])).astype(jnp.int32)
    return place, code


def head_at(code, place):
    return lax.bitwise_and(lax.shift_right_logical(code, 3 * place), 7) - 1


def columns_of(head):
    return pl.ds(pl.multiple_of(head * HS, HS), HS)


def pack_kernel(student_ref, target_ref, *refs):
    slots, sems = in_slot_order(refs, ROUNDS_IN), refs[GROUP]
    place, code = place_and_code()

    def copies(k, head):
        return [
            pltpu.make_async_copy(
                view.at[:, :, columns_of(head)], slots[k].at[pl.ds(3 * i, 3)], sems.at[k, i]
            )
            for i, view in enumerate((student_ref, target_ref))
        ]

    for step in ("start", "wait"):
        for k in ROUNDS_IN + (0,):
            head = head_at(code, lax.bitwise_xor(place, k))

            @pl.when(head >= 0)
            def _():
                for copy in copies(k, head):
                    copy.start() if step == "start" else copy.wait()


def in_slot_order(refs, rounds):
    return [refs[((0,) + rounds).index(k)] for k in range(GROUP)]


def head_kernel(clip_count, extra, lengths_ref, *refs):
    slots = in_slot_order(refs, ROUNDS_IN) + list(refs[GROUP : GROUP + extra])
    refs = refs[GROUP + extra :]
    outs = in_slot_order(refs, ROUNDS_OUT) + list(refs[GROUP : GROUP + extra])
    data, turned, grads, totals_ref = refs[GROUP + extra :]
    place, code = place_and_code()
    rows = slots[0].shape[1]
    scale = 1.0 / math.sqrt(HS)
    to_log2 = scale * math.log2(math.e)
    totals_ref[...] = jnp.zeros_like(totals_ref)
    clip_rows = totals_ref.shape[0]
    outs[0][4 * rows :] = jnp.zeros((2 * clip_rows, HS), BF16)

    def rows_of(slot):
        block = lax.bitwise_xor(place, slot) if slot < GROUP else slot
        return pl.ds(pl.multiple_of(block * rows, rows), rows)

    def clip_pass(blocks, clip, start, length):
        size = blocks * LANES
        first = pl.multiple_of(lax.div(start, LANES) * LANES, LANES)
        window = pl.ds(first, size)
        start = start - first
        query_column = lax.broadcasted_iota(jnp.int32, (1, size), 1)
        inside = (query_column >= start) & (query_column < start + length)

        def masked(scores, axis):
            parts = jnp.split(scores, blocks, axis=axis)
            for i in sorted({0, blocks - 1}):
                shape = (1, LANES) if axis == 1 else (LANES, LANES)
                key = lax.broadcasted_iota(jnp.int32, shape, axis) + i * LANES
                bias = jnp.where((key >= start) & (key < start + length), 0.0, -jnp.inf)
                if axis == 0:
                    bias = jnp.concatenate([bias] * (scores.shape[1] // LANES), axis=1)
                parts[i] = parts[i] + bias
            return jnp.concatenate(parts, axis=axis)

        def powers(scores, axis):
            peak = jnp.max(scores, axis=axis, keepdims=True)
            return jnp.exp2((scores - peak) * to_log2)

        def product(a, b):
            return lax.dot_general(a, b, ROWS_BY_ROWS, preferred_element_type=F32)

        dkey = dvalue = total = None
        for begin in range(0, size, QUERY_TILE):
            width = min(QUERY_TILE, size - begin)
            mine = pl.ds(first + begin, width)
            columns = slice(begin, begin + width)
            exponent = powers(masked(product(data[3, mine, :], data[4, window, :]), 1), 1)
            values = jnp.concatenate([data[5, window, :], jnp.ones((size, HS), BF16)], axis=1)
            both = jnp.dot(exponent.astype(BF16), values, preferred_element_type=F32)
            target = both[:, :HS] * (1.0 / both[:, HS:])
            exponent = powers(masked(product(data[1, window, :], data[0, mine, :]), 0), 0)
            weights = exponent.astype(BF16)
            inverse = 1.0 / jnp.sum(exponent, axis=0, keepdims=True)
            student = jnp.dot(turned[1, :, window], weights, preferred_element_type=F32) * inverse
            diff = jnp.where(inside[:, columns], student - target.T, 0.0)
            squares = jnp.sum(diff * diff, axis=1, keepdims=True)
            total = squares if total is None else total + squares
            gradient = (diff * inverse).astype(BF16)
            delta = jnp.sum(gradient.astype(F32) * student, axis=0, keepdims=True)
            slope = jnp.dot(data[2, window, :], gradient, preferred_element_type=F32)
            dscores = (exponent * (slope - delta)).astype(BF16)
            dquery = jnp.dot(turned[0, :, window], dscores, preferred_element_type=F32)
            key_part = jnp.dot(dscores, data[0, mine, :], preferred_element_type=F32)
            value_part = product(weights, gradient)
            grads[0, mine, :] += (dquery * scale).T
            parts = jnp.split(target, width // LANES, axis=0)
            for i in {0, blocks - 1} & {i + begin // LANES for i in range(width // LANES)}:
                query = lax.broadcasted_iota(jnp.int32, (LANES, HS), 0) + i * LANES
                keep = (query >= start) & (query < start + length)
                i = i - begin // LANES
                parts[i] = jnp.where(keep, parts[i], 0.0)
            grads[3, mine, :] += jnp.concatenate(parts, axis=0)
            dkey = key_part if dkey is None else dkey + key_part
            dvalue = value_part if dvalue is None else dvalue + value_part
        grads[1, window, :] += dkey * scale
        grads[2, window, :] += dvalue
        clip_iota = lax.broadcasted_iota(jnp.int32, (clip_rows, 1), 0)
        total = jnp.sum(total, axis=0, keepdims=True)
        totals_ref[...] += jnp.where(clip_iota == clip, total, 0.0)

    @pl.when(head_at(code, place) >= 0)
    def _():
        group_start = lax.div(lax.axis_index("seq"), GROUP) * (GROUP * rows)
        for slot in range(GROUP + extra):
            where = rows_of(slot)
            for part in range(6):
                data[part, where, :] = slots[slot][part]
            for turn, part in enumerate((1, 2)):
                turned[turn, :, where] = slots[slot][part].T
        grads[...] = jnp.zeros_like(grads)

        def one_clip(clip, begin):
            length = lengths_ref[clip]
            start = begin - group_start

            @pl.when((start >= 0) & (start < GROUP * rows))
            def _():
                lead = lax.rem(start, LANES)
                blocks = lax.div(lead + length + LANES - 1, LANES)
                for count in range(1, MOST // LANES + 2):

                    @pl.when(blocks == count)
                    def _():
                        clip_pass(count, clip, start, length)

            return begin + length

        lax.fori_loop(0, clip_count, one_clip, jnp.int32(0))
        high = totals_ref[...].astype(BF16)
        low = (totals_ref[...] - high.astype(F32)).astype(BF16)
        for slot in range(GROUP + extra):
            where = rows_of(slot)
            for part in range(4):
                outs[slot][part * rows : (part + 1) * rows] = grads[part, where, :].astype(BF16)
            outs[slot][4 * rows : 4 * rows + clip_rows] = high
            outs[slot][4 * rows + clip_rows :] = low


def sum_kernel(*refs):
    out = refs[-1]
    clip_rows = out.shape[0]
    total = jnp.zeros(out.shape, F32)
    for slot in refs[:-1]:
        start = slot.shape[0] - 2 * clip_rows
        total = total + slot[start : start + clip_rows].astype(F32)
        total = total + slot[start + clip_rows :].astype(F32)
    out[...] = total


def finish_kernel(clip_count, head_count, extra, sec_count, lengths_ref, *refs):
    sums, refs = refs[:sec_count], refs[sec_count:]
    slots, extras = in_slot_order(refs, ROUNDS_OUT), refs[GROUP:-5]
    grads_out, target_out, grads_ref, target_ref, sems = refs[-5:]
    place, code = place_and_code()
    rows = target_ref.shape[0]
    totals = sum((ref[...] for ref in sums[1:]), sums[0][...])
    first = lax.axis_index("seq") * rows
    token = first + lax.broadcasted_iota(jnp.int32, (rows, HS), 0)
    factor = jnp.zeros((rows, HS), F32)
    begin = jnp.int32(0)
    for clip in range(clip_count):
        length = lengths_ref[clip]
        size = length.astype(F32) * (H * HS)
        value = lax.rsqrt(totals[clip : clip + 1, :] / size + EPS)
        factor = jnp.where((token >= begin) & (token < begin + length), value, factor)
        begin = begin + length
    def for_heads(visit):
        for k in range(GROUP):
            head = head_at(code, lax.bitwise_xor(place, k))
            pl.when(head >= 0)(functools.partial(visit, k, columns_of(head)))

    def copies(k, cols):
        return (
            pltpu.make_async_copy(
                grads_ref.at[:, :, cols], grads_out.at[:, :, cols], sems.at[k, 0]
            ),
            pltpu.make_async_copy(target_ref.at[:, cols], target_out.at[:, cols], sems.at[k, 1]),
        )

    def start(k, cols):
        for copy in copies(k, cols):
            copy.start()

    def wait(k, cols):
        for copy in copies(k, cols):
            copy.wait()

    def scale(k, cols):
        target_ref[:, cols] = slots[k][3 * rows : 4 * rows]
        for part in range(3):
            block = slots[k][part * rows : (part + 1) * rows].astype(F32)
            grads_ref[part, :, cols] = (block * factor).astype(BF16)
        if not extra:
            start(k, cols)

    for_heads(scale)
    for head in range(head_count if extra else 0):
        cols = slice(head * HS, (head + 1) * HS)
        for part in range(3):
            more = extras[head][part * rows : (part + 1) * rows].astype(F32)
            more = (more * factor).astype(BF16)
            grads_ref[part, :, cols] = grads_ref[part, :, cols] + more
        target_ref[:, cols] = target_ref[:, cols] + extras[head][3 * rows : 4 * rows]
    if extra:
        for_heads(start)
    for_heads(wait)


def both_axes(sec_count, seq_count, pairs_of):
    pairs = []
    for sec in range(sec_count):
        for start in range(0, seq_count, GROUP):
            for source, target in pairs_of(OWNERS[sec % 2], start):
                if source < seq_count and target < seq_count:
                    pairs.append((sec * seq_count + source, sec * seq_count + target))
    return pairs


def per_device(sec_count, seq_count, student_qkv, target_qkv, clip_lengths):
    rows, _, width = student_qkv.shape
    head_count = width // HS
    clip_count = clip_lengths.shape[0]
    clip_rows = -(-clip_count // 8) * 8
    extra = MOST // rows if seq_count > GROUP else 0
    axes = ("sec", "seq")
    pairs = functools.partial(both_axes, sec_count, seq_count)
    small = pltpu.CompilerParams(vmem_limit_bytes=SMALL_VMEM)

    packed = pl.pallas_call(
        pack_kernel,
        out_shape=[jax.ShapeDtypeStruct((6, rows, HS), BF16)] * GROUP,
        in_specs=[pl.BlockSpec(memory_space=pltpu.HBM)] * 2,
        out_specs=[VMEM] * GROUP,
        scratch_shapes=[pltpu.SemaphoreType.DMA((GROUP, 2))],
        compiler_params=small,
        name="pack",
    )(
        pltpu.with_memory_space_constraint(jnp.transpose(student_qkv, (1, 0, 2)), pltpu.HBM),
        pltpu.with_memory_space_constraint(jnp.transpose(target_qkv, (1, 0, 2)), pltpu.HBM),
    )

    gathered = [packed[0]]
    for k, mine in zip(ROUNDS_IN, packed[1:]):
        gathered.append(
            lax.ppermute(
                mine, axes, pairs(lambda owners, start: [(start + (d ^ k), start + d) for d in owners])
            )
        )
    for block in range(extra):
        pieces = []
        for head in range(head_count):
            cols = slice(head * HS, (head + 1) * HS)
            piece = jnp.concatenate([student_qkv[:, :, cols], target_qkv[:, :, cols]], axis=1)
            pieces.append(
                lax.ppermute(
                    jnp.transpose(piece, (1, 0, 2)),
                    axes,
                    pairs(lambda owners, start: [(start + GROUP + block, start + owners[head])]),
                )
            )
        gathered.append(sum(pieces[1:], pieces[0]))

    tokens = (GROUP + extra) * rows
    payload = jax.ShapeDtypeStruct((4 * rows + 2 * clip_rows, HS), BF16)
    results = pl.pallas_call(
        functools.partial(head_kernel, clip_count, extra),
        out_shape=[payload] * (GROUP + extra),
        in_specs=[SMEM] + [VMEM] * (GROUP + extra),
        out_specs=[VMEM] * (GROUP + extra),
        scratch_shapes=[
            pltpu.VMEM((6, tokens, HS), BF16),
            pltpu.VMEM((2, HS, tokens), BF16),
            pltpu.VMEM((4, tokens, HS), F32),
            pltpu.VMEM((clip_rows, HS), F32),
        ],
        compiler_params=pltpu.CompilerParams(vmem_limit_bytes=HEADS_VMEM),
        name="heads",
    )(clip_lengths, *gathered)

    returned = [results[0]]
    for k, mine in zip(ROUNDS_OUT, results[1:]):
        returned.append(
            lax.ppermute(
                mine, axes, pairs(lambda owners, start: [(start + d, start + (d ^ k)) for d in owners])
            )
        )
    extras = []
    for head in range(head_count if extra else 0):
        pieces = [
            lax.ppermute(
                results[GROUP + block],
                axes,
                pairs(lambda owners, start: [(start + owners[head], start + GROUP + block)]),
            )
            for block in range(extra)
        ]
        extras.append(sum(pieces[1:], pieces[0]))
    totals = pl.pallas_call(
        sum_kernel,
        out_shape=jax.ShapeDtypeStruct((clip_rows, HS), F32),
        in_specs=[VMEM] * GROUP,
        out_specs=VMEM,
        compiler_params=small,
        name="totals",
    )(*returned)

    def over(totals, axis, count, step):
        return lax.ppermute(totals, axis, [(s, s ^ step) for s in range(count)])

    step = GROUP
    while step < seq_count:
        totals = totals + over(totals, "seq", seq_count, step)
        step *= 2
    others = [over(totals, "sec", sec_count, step) for step in range(1, sec_count)]

    grads, target_out = pl.pallas_call(
        functools.partial(finish_kernel, clip_count, head_count, extra, sec_count),
        out_shape=[
            jax.ShapeDtypeStruct((3, rows, width), BF16),
            jax.ShapeDtypeStruct((rows, width), BF16),
        ],
        in_specs=[SMEM] + [VMEM] * (sec_count + GROUP + len(extras)),
        out_specs=[pl.BlockSpec(memory_space=pltpu.HBM)] * 2,
        scratch_shapes=[
            pltpu.VMEM((3, rows, width), BF16),
            pltpu.VMEM((rows, width), BF16),
            pltpu.SemaphoreType.DMA((GROUP, 2)),
        ],
        compiler_params=small,
        name="finish",
    )(clip_lengths, totals, *others, *returned, *extras)
    return jnp.transpose(grads, (1, 0, 2)), target_out


def solution(mesh):
    return jax.shard_map(
        functools.partial(per_device, mesh.shape["sec"], mesh.shape["seq"]),
        mesh=mesh,
        in_specs=(P("seq", None, "sec"), P("seq", None, "sec"), P()),
        out_specs=(P("seq", None, "sec"), P("seq", "sec")),
        check_vma=False,
    )
```

```python
import functools
import math

import jax
import jax.numpy as jnp
from jax import lax
from jax.experimental import pallas as pl
from jax.experimental.pallas import tpu as pltpu
from jax.sharding import PartitionSpec as P

H = 20
HS = 128
MOST = 384
EPS = 1e-05

GROUP = 8
OWNERS = ((0, 2, 4, 5, 7), (1, 2, 3, 5, 6))
ROUNDS_IN = (4, 3, 5, 1, 7, 6, 2)
ROUNDS_OUT = (7, 3, 5, 4, 2, 6, 1)
QUERY_TILE = 512
LANES = 128
HEADS_VMEM = 40 * 1024 * 1024
SMALL_VMEM = 8 * 1024 * 1024

BF16 = jnp.bfloat16
F32 = jnp.float32
ROWS_BY_ROWS = (((1,), (1,)), ((), ()))
VMEM = pl.BlockSpec(memory_space=pltpu.VMEM)
SMEM = pl.BlockSpec(memory_space=pltpu.SMEM)


def owner_code(owners):
    return sum((head + 1) << (3 * place) for head, place in enumerate(owners))


def place_and_code():
    place = lax.rem(lax.axis_index("seq"), GROUP)
    odd = lax.rem(lax.axis_index("sec"), 2) == 1
    code = jnp.where(odd, owner_code(OWNERS[1]), owner_code(OWNERS[0])).astype(jnp.int32)
    return place, code


def head_at(code, place):
    return lax.bitwise_and(lax.shift_right_logical(code, 3 * place), 7) - 1


def columns_of(head):
    return pl.ds(pl.multiple_of(head * HS, HS), HS)


def pack_kernel(student_ref, target_ref, *refs):
    slots, sems = in_slot_order(refs, ROUNDS_IN), refs[GROUP]
    place, code = place_and_code()

    def copies(k, head):
        return [
            pltpu.make_async_copy(
                view.at[:, :, columns_of(head)], slots[k].at[pl.ds(3 * i, 3)], sems.at[k, i]
            )
            for i, view in enumerate((student_ref, target_ref))
        ]

    for step in ("start", "wait"):
        for k in ROUNDS_IN + (0,):
            head = head_at(code, lax.bitwise_xor(place, k))

            @pl.when(head >= 0)
            def _():
                for copy in copies(k, head):
                    copy.start() if step == "start" else copy.wait()


def in_slot_order(refs, rounds):
    return [refs[((0,) + rounds).index(k)] for k in range(GROUP)]


def head_kernel(clip_count, extra, lengths_ref, *refs):
    slots = in_slot_order(refs, ROUNDS_IN) + list(refs[GROUP : GROUP + extra])
    refs = refs[GROUP + extra :]
    outs = in_slot_order(refs, ROUNDS_OUT) + list(refs[GROUP : GROUP + extra])
    data, turned, grads, totals_ref = refs[GROUP + extra :]
    place, code = place_and_code()
    rows = slots[0].shape[1]
    scale = 1.0 / math.sqrt(HS)
    to_log2 = scale * math.log2(math.e)
    totals_ref[...] = jnp.zeros_like(totals_ref)
    clip_rows = totals_ref.shape[0]
    outs[0][4 * rows :] = jnp.zeros((2 * clip_rows, HS), BF16)

    def rows_of(slot):
        block = lax.bitwise_xor(place, slot) if slot < GROUP else slot
        return pl.ds(pl.multiple_of(block * rows, rows), rows)

    def clip_pass(blocks, clip, start, length):
        size = blocks * LANES
        first = pl.multiple_of(lax.div(start, LANES) * LANES, LANES)
        window = pl.ds(first, size)
        start = start - first
        query_column = lax.broadcasted_iota(jnp.int32, (1, size), 1)
        inside = (query_column >= start) & (query_column < start + length)

        def masked(scores, axis):
            parts = jnp.split(scores, blocks, axis=axis)
            for i in sorted({0, blocks - 1}):
                shape = (1, LANES) if axis == 1 else (LANES, LANES)
                key = lax.broadcasted_iota(jnp.int32, shape, axis) + i * LANES
                bias = jnp.where((key >= start) & (key < start + length), 0.0, -jnp.inf)
                if axis == 0:
                    bias = jnp.concatenate([bias] * (scores.shape[1] // LANES), axis=1)
                parts[i] = parts[i] + bias
            return jnp.concatenate(parts, axis=axis)

        def powers(scores, axis):
            peak = jnp.max(scores, axis=axis, keepdims=True)
            return jnp.exp2((scores - peak) * to_log2)

        def product(a, b):
            return lax.dot_general(a, b, ROWS_BY_ROWS, preferred_element_type=F32)

        tiles = range(0, size, QUERY_TILE)
        widths = [min(QUERY_TILE, size - begin) for begin in tiles]
        mines = [pl.ds(first + begin, width) for begin, width in zip(tiles, widths)]
        insides = [inside[:, begin : begin + width] for begin, width in zip(tiles, widths)]
        values = jnp.concatenate([data[5, window, :], jnp.ones((size, HS), BF16)], axis=1)

        def each(function, *lists):
            return [function(*items) for items in zip(*lists)]

        target_scores = each(lambda mine: product(data[3, mine, :], data[4, window, :]), mines)
        student_scores = each(lambda mine: product(data[1, window, :], data[0, mine, :]), mines)
        mixed = each(lambda scores: powers(masked(scores, 1), 1).astype(BF16), target_scores)
        exponents = each(lambda scores: powers(masked(scores, 0), 0), student_scores)
        boths = each(lambda a: jnp.dot(a, values, preferred_element_type=F32), mixed)
        targets = each(lambda both: both[:, :HS] * (1.0 / both[:, HS:]), boths)
        weights = each(lambda exponent: exponent.astype(BF16), exponents)
        inverses = each(lambda e: 1.0 / jnp.sum(e, axis=0, keepdims=True), exponents)
        outs_t = each(
            lambda a: jnp.dot(turned[1, :, window], a, preferred_element_type=F32), weights
        )
        students = each(lambda out, inverse: out * inverse, outs_t, inverses)
        diffs = each(
            lambda s, o, keep: jnp.where(keep, s - o.T, 0.0), students, targets, insides
        )
        total = sum(each(lambda diff: jnp.sum(diff * diff, axis=1, keepdims=True), diffs))
        gradients = each(lambda diff, inverse: (diff * inverse).astype(BF16), diffs, inverses)
        deltas = each(
            lambda g, s: jnp.sum(g.astype(F32) * s, axis=0, keepdims=True), gradients, students
        )
        slopes = each(
            lambda g: jnp.dot(data[2, window, :], g, preferred_element_type=F32), gradients
        )
        dscores = each(lambda e, s, d: (e * (s - d)).astype(BF16), exponents, slopes, deltas)
        dqueries = each(
            lambda d: jnp.dot(turned[0, :, window], d, preferred_element_type=F32), dscores
        )
        dkey = sum(
            each(
                lambda d, mine: jnp.dot(d, data[0, mine, :], preferred_element_type=F32), dscores, mines
            )
        )
        dvalue = sum(each(product, weights, gradients))
        for begin, width, mine, dquery, target in zip(tiles, widths, mines, dqueries, targets):
            grads[0, mine, :] += (dquery * scale).T
            query = lax.broadcasted_iota(jnp.int32, (width, HS), 0) + begin
            grads[3, mine, :] += jnp.where((query >= start) & (query < start + length), target, 0.0)
        grads[1, window, :] += dkey * scale
        grads[2, window, :] += dvalue
        clip_iota = lax.broadcasted_iota(jnp.int32, (clip_rows, 1), 0)
        total = jnp.sum(total, axis=0, keepdims=True)
        totals_ref[...] += jnp.where(clip_iota == clip, total, 0.0)

    @pl.when(head_at(code, place) >= 0)
    def _():
        group_start = lax.div(lax.axis_index("seq"), GROUP) * (GROUP * rows)
        for slot in range(GROUP + extra):
            where = rows_of(slot)
            for part in range(6):
                data[part, where, :] = slots[slot][part]
            for turn, part in enumerate((1, 2)):
                turned[turn, :, where] = slots[slot][part].T
        grads[...] = jnp.zeros_like(grads)

        def one_clip(clip, begin):
            length = lengths_ref[clip]
            start = begin - group_start

            @pl.when((start >= 0) & (start < GROUP * rows))
            def _():
                lead = lax.rem(start, LANES)
                blocks = lax.div(lead + length + LANES - 1, LANES)
                for count in range(1, MOST // LANES + 2):

                    @pl.when(blocks == count)
                    def _():
                        clip_pass(count, clip, start, length)

            return begin + length

        lax.fori_loop(0, clip_count, one_clip, jnp.int32(0))
        high = totals_ref[...].astype(BF16)
        low = (totals_ref[...] - high.astype(F32)).astype(BF16)
        for slot in range(GROUP + extra):
            where = rows_of(slot)
            for part in range(4):
                outs[slot][part * rows : (part + 1) * rows] = grads[part, where, :].astype(BF16)
            outs[slot][4 * rows : 4 * rows + clip_rows] = high
            outs[slot][4 * rows + clip_rows :] = low


def sum_kernel(*refs):
    out = refs[-1]
    clip_rows = out.shape[0]
    total = jnp.zeros(out.shape, F32)
    for slot in refs[:-1]:
        start = slot.shape[0] - 2 * clip_rows
        total = total + slot[start : start + clip_rows].astype(F32)
        total = total + slot[start + clip_rows :].astype(F32)
    out[...] = total


def finish_kernel(clip_count, head_count, extra, sec_count, lengths_ref, *refs):
    sums, refs = refs[:sec_count], refs[sec_count:]
    slots, extras = in_slot_order(refs, ROUNDS_OUT), refs[GROUP:-5]
    grads_out, target_out, grads_ref, target_ref, sems = refs[-5:]
    place, code = place_and_code()
    rows = target_ref.shape[0]
    totals = sum((ref[...] for ref in sums[1:]), sums[0][...])
    first = lax.axis_index("seq") * rows
    token = first + lax.broadcasted_iota(jnp.int32, (rows, HS), 0)
    factor = jnp.zeros((rows, HS), F32)
    begin = jnp.int32(0)
    for clip in range(clip_count):
        length = lengths_ref[clip]
        size = length.astype(F32) * (H * HS)
        value = lax.rsqrt(totals[clip : clip + 1, :] / size + EPS)
        factor = jnp.where((token >= begin) & (token < begin + length), value, factor)
        begin = begin + length
    def for_heads(visit):
        for k in range(GROUP):
            head = head_at(code, lax.bitwise_xor(place, k))
            pl.when(head >= 0)(functools.partial(visit, k, columns_of(head)))

    def copies(k, cols):
        return (
            pltpu.make_async_copy(
                grads_ref.at[:, :, cols], grads_out.at[:, :, cols], sems.at[k, 0]
            ),
            pltpu.make_async_copy(target_ref.at[:, cols], target_out.at[:, cols], sems.at[k, 1]),
        )

    def start(k, cols):
        for copy in copies(k, cols):
            copy.start()

    def wait(k, cols):
        for copy in copies(k, cols):
            copy.wait()

    def scale(k, cols):
        target_ref[:, cols] = slots[k][3 * rows : 4 * rows]
        for part in range(3):
            block = slots[k][part * rows : (part + 1) * rows].astype(F32)
            grads_ref[part, :, cols] = (block * factor).astype(BF16)
        if not extra:
            start(k, cols)

    for_heads(scale)
    for head in range(head_count if extra else 0):
        cols = slice(head * HS, (head + 1) * HS)
        for part in range(3):
            more = extras[head][part * rows : (part + 1) * rows].astype(F32)
            more = (more * factor).astype(BF16)
            grads_ref[part, :, cols] = grads_ref[part, :, cols] + more
        target_ref[:, cols] = target_ref[:, cols] + extras[head][3 * rows : 4 * rows]
    if extra:
        for_heads(start)
    for_heads(wait)


def both_axes(sec_count, seq_count, pairs_of):
    pairs = []
    for sec in range(sec_count):
        for start in range(0, seq_count, GROUP):
            for source, target in pairs_of(OWNERS[sec % 2], start):
                if source < seq_count and target < seq_count:
                    pairs.append((sec * seq_count + source, sec * seq_count + target))
    return pairs


def per_device(sec_count, seq_count, student_qkv, target_qkv, clip_lengths):
    rows, _, width = student_qkv.shape
    head_count = width // HS
    clip_count = clip_lengths.shape[0]
    clip_rows = -(-clip_count // 8) * 8
    extra = MOST // rows if seq_count > GROUP else 0
    axes = ("sec", "seq")
    pairs = functools.partial(both_axes, sec_count, seq_count)
    small = pltpu.CompilerParams(vmem_limit_bytes=SMALL_VMEM)

    packed = pl.pallas_call(
        pack_kernel,
        out_shape=[jax.ShapeDtypeStruct((6, rows, HS), BF16)] * GROUP,
        in_specs=[pl.BlockSpec(memory_space=pltpu.HBM)] * 2,
        out_specs=[VMEM] * GROUP,
        scratch_shapes=[pltpu.SemaphoreType.DMA((GROUP, 2))],
        compiler_params=small,
        name="pack",
    )(
        pltpu.with_memory_space_constraint(jnp.transpose(student_qkv, (1, 0, 2)), pltpu.HBM),
        pltpu.with_memory_space_constraint(jnp.transpose(target_qkv, (1, 0, 2)), pltpu.HBM),
    )

    gathered = [packed[0]]
    for k, mine in zip(ROUNDS_IN, packed[1:]):
        gathered.append(
            lax.ppermute(
                mine, axes, pairs(lambda owners, start: [(start + (d ^ k), start + d) for d in owners])
            )
        )
    for block in range(extra):
        pieces = []
        for head in range(head_count):
            cols = slice(head * HS, (head + 1) * HS)
            piece = jnp.concatenate([student_qkv[:, :, cols], target_qkv[:, :, cols]], axis=1)
            pieces.append(
                lax.ppermute(
                    jnp.transpose(piece, (1, 0, 2)),
                    axes,
                    pairs(lambda owners, start: [(start + GROUP + block, start + owners[head])]),
                )
            )
        gathered.append(sum(pieces[1:], pieces[0]))

    tokens = (GROUP + extra) * rows
    payload = jax.ShapeDtypeStruct((4 * rows + 2 * clip_rows, HS), BF16)
    results = pl.pallas_call(
        functools.partial(head_kernel, clip_count, extra),
        out_shape=[payload] * (GROUP + extra),
        in_specs=[SMEM] + [VMEM] * (GROUP + extra),
        out_specs=[VMEM] * (GROUP + extra),
        scratch_shapes=[
            pltpu.VMEM((6, tokens, HS), BF16),
            pltpu.VMEM((2, HS, tokens), BF16),
            pltpu.VMEM((4, tokens, HS), F32),
            pltpu.VMEM((clip_rows, HS), F32),
        ],
        compiler_params=pltpu.CompilerParams(vmem_limit_bytes=HEADS_VMEM),
        name="heads",
    )(clip_lengths, *gathered)

    returned = [results[0]]
    for k, mine in zip(ROUNDS_OUT, results[1:]):
        returned.append(
            lax.ppermute(
                mine, axes, pairs(lambda owners, start: [(start + d, start + (d ^ k)) for d in owners])
            )
        )
    extras = []
    for head in range(head_count if extra else 0):
        pieces = [
            lax.ppermute(
                results[GROUP + block],
                axes,
                pairs(lambda owners, start: [(start + owners[head], start + GROUP + block)]),
            )
            for block in range(extra)
        ]
        extras.append(sum(pieces[1:], pieces[0]))
    totals = pl.pallas_call(
        sum_kernel,
        out_shape=jax.ShapeDtypeStruct((clip_rows, HS), F32),
        in_specs=[VMEM] * GROUP,
        out_specs=VMEM,
        compiler_params=small,
        name="totals",
    )(*returned)

    def over(totals, axis, count, step):
        return lax.ppermute(totals, axis, [(s, s ^ step) for s in range(count)])

    step = GROUP
    while step < seq_count:
        totals = totals + over(totals, "seq", seq_count, step)
        step *= 2
    others = [over(totals, "sec", sec_count, step) for step in range(1, sec_count)]

    grads, target_out = pl.pallas_call(
        functools.partial(finish_kernel, clip_count, head_count, extra, sec_count),
        out_shape=[
            jax.ShapeDtypeStruct((3, rows, width), BF16),
            jax.ShapeDtypeStruct((rows, width), BF16),
        ],
        in_specs=[SMEM] + [VMEM] * (sec_count + GROUP + len(extras)),
        out_specs=[pl.BlockSpec(memory_space=pltpu.HBM)] * 2,
        scratch_shapes=[
            pltpu.VMEM((3, rows, width), BF16),
            pltpu.VMEM((rows, width), BF16),
            pltpu.SemaphoreType.DMA((GROUP, 2)),
        ],
        compiler_params=small,
        name="finish",
    )(clip_lengths, totals, *others, *returned, *extras)
    return jnp.transpose(grads, (1, 0, 2)), target_out


def solution(mesh):
    return jax.shard_map(
        functools.partial(per_device, mesh.shape["sec"], mesh.shape["seq"]),
        mesh=mesh,
        in_specs=(P("seq", None, "sec"), P("seq", None, "sec"), P()),
        out_specs=(P("seq", None, "sec"), P("seq", "sec")),
        check_vma=False,
    )
```
